256 devices in a mesh: grp: 8 (over x, z_lo), shard: 32 (over z_hi, y, core).
Axes of the slice: x: 4, y: 4, z: 8 (z_hi: 4, z_lo: 2; z = z_hi * 2 + z_lo), core: 2. Of those that a mesh axis runs over, the one named last changes fastest.
Arguments:
- voltages: bfloat16 [16, 4194304], P('grp', 'shard'), may hold values from -6 to 6
- eq_gain: float32 [16, 4096], P('grp'), may hold values from 0.5 to 2
- delays: float32 [1024, 16], replicated, may hold values from -16 to 16
Outputs:
- beam_power: bfloat16 [32, 8, 4096, 1024], P(None, 'grp', 'shard')
The draws below stay inside these ranges and needn't reach their ends.
All inputs are finite; a program needn't handle non-finite values.
Results may differ from the reference program's by a relative error of at most 0.0054.
Values may be sent and summed in bfloat16 or wider, within the bound.
No kernel may reach another device: no remote copies, remote signals or barrier semaphores. Data moves between devices by JAX's collectives and lax.ppermute only.
A program may use at most 256 MiB of HBM per device.

```python
import math
import jax
import jax.numpy as jnp
from jax import lax

CHANNELS = 4096
TAPS = 16
INTEG = 2
BEAMS = 1024
SPEC_DEV = 16
INPUTS = 16
SAMPLES = 4194304


def block_scale(stream_key, extent, cuts, smallest, top_value):
    def one(position, parts):
        draws = jax.random.uniform(jax.random.fold_in(jax.random.fold_in(stream_key, 6), position), (parts,), jnp.float32, smallest / len(cuts), top_value / len(cuts))
        return jnp.repeat(jnp.exp(draws), extent[position] // parts).reshape((-1,) + (1,) * (len(extent) - position - 1))

    level = one(*cuts[0])
    for cut in cuts[1:]:
        level = level * one(*cut)
    return level


def gaussian(rng, dims, width, limit, shards=(), kind=jnp.bfloat16):
    array = jax.random.normal(rng, dims, jnp.float32) * width
    if len(shards) > 0:
        array = block_scale(rng, dims, shards, -0.22, 0.18) * array
    return jnp.clip(array, min=-limit, max=limit).astype(kind)


def setup_inputs(seed: int = 0) -> dict:
    seeds = jax.random.split(jax.random.key(seed), 4)
    voltages = gaussian(seeds[0], (INPUTS, SAMPLES), 1.0, 6.0, ((0, 8), (1, 32)))
    eq_gain = jnp.clip(jnp.exp(math.log(2.0) - 1.3862944 * jax.random.uniform(seeds[1], (INPUTS, CHANNELS), jnp.float32) ** block_scale(seeds[1], (INPUTS, CHANNELS), ((0, 8),), -0.2, 0.2)), 0.5, 2.0)
    delays = jnp.clip(jax.random.uniform(seeds[2], (BEAMS, INPUTS), jnp.float32, -16.0, 16.0), -16.0, 16.0)
    return {"voltages": voltages, "eq_gain": eq_gain, "delays": delays}


def make_window(tap_count, length):
    total = tap_count * length
    places = jnp.arange(total).astype(jnp.float32)
    centred = (places - (total - 1) / 2.0) / length
    taper = 0.5 - 0.5 * jnp.cos(2.0 * math.pi / total * (places + 0.5))
    shaped = jnp.sinc(centred) * taper
    shaped = shaped / jnp.sqrt(jnp.sum(shaped * shaped))
    return shaped.reshape(tap_count, length)

def input_spectra(samples, gain_row, window):
    length = 2 * CHANNELS
    frames = samples.astype(jnp.float32).reshape(-1, length)
    frame_count = frames.shape[0]
    padded = jnp.concatenate([jnp.zeros((TAPS - 1, length), jnp.float32), frames], axis=0)
    filtered = jnp.zeros((frame_count, length), jnp.float32)
    for tap_index in range(TAPS):
        filtered = filtered + window[tap_index][None, :] * padded[tap_index:tap_index + frame_count]
    spectrum = jnp.fft.rfft(filtered, axis=1)[:, :CHANNELS]
    real_part = (jnp.real(spectrum) * gain_row[None, :]).astype(jnp.bfloat16)
    imag_part = (jnp.imag(spectrum) * gain_row[None, :]).astype(jnp.bfloat16)
    return jnp.stack([real_part, imag_part])

def beam_block(spectra, delays, first_chan, span):
    piece = lax.dynamic_slice_in_dim(spectra, first_chan.astype(jnp.int32), span, 3).astype(jnp.float32)
    chan_index = first_chan.astype(jnp.int32) + jnp.arange(span, dtype=jnp.int32)
    factor = 1.0 + chan_index.astype(jnp.float32) / CHANNELS
    phases = 2.0 * math.pi * (delays[:, :, None] * factor[None, None, :])
    w_real = jnp.cos(phases).astype(jnp.bfloat16)
    w_imag = (-jnp.sin(phases)).astype(jnp.bfloat16)
    w_real = lax.optimization_barrier(w_real).astype(jnp.float32)
    w_imag = lax.optimization_barrier(w_imag).astype(jnp.float32)
    beam_real = jnp.einsum('itk,bik->tkb', piece[:, 0], w_real) - jnp.einsum('itk,bik->tkb', piece[:, 1], w_imag)
    beam_imag = jnp.einsum('itk,bik->tkb', piece[:, 0], w_imag) + jnp.einsum('itk,bik->tkb', piece[:, 1], w_real)
    intensity = beam_real * beam_real + beam_imag * beam_imag
    total_spec = intensity.shape[0]
    intensity = intensity.reshape(total_spec // SPEC_DEV, SPEC_DEV // INTEG, INTEG, span, BEAMS).sum(axis=2)
    return (intensity / INPUTS).astype(jnp.bfloat16)

def reference(voltages, eq_gain, delays):
    window = make_window(TAPS, 2 * CHANNELS)

    def one_input(item_pair):
        return input_spectra(item_pair[0], item_pair[1], window)
    spectra = lax.map(one_input, (voltages, eq_gain))
    span = min(64, CHANNELS)
    starts = (jnp.arange(CHANNELS // span) * span).astype(jnp.int32)

    def one_block(first_chan):
        return beam_block(spectra, delays, first_chan, span)
    results = lax.map(one_block, starts)
    ordered = jnp.transpose(results, (1, 2, 0, 3, 4))
    return ordered.reshape(results.shape[1], results.shape[2], CHANNELS, BEAMS)
```

```python
import math

import jax
import jax.numpy as jnp
import numpy as np
from jax import lax
from jax.experimental import pallas as pl
from jax.experimental.pallas import tpu as pltpu
from jax.sharding import PartitionSpec as P

CHANNELS = 4096
TAPS = 16
INPUTS = 16
LENGTH = 2 * CHANNELS
INNER = 64
LANES = 128
F32 = jnp.float32
BF16 = jnp.bfloat16


def shifted(value, axis, steps):
    count = lax.axis_size(axis)
    initial, last = (max(0, -steps), min(count, count - steps))
    return lax.ppermute(value, axis, [(source, source + steps) for source in range(initial, last)])


def split(values):
    high = values.astype(np.float32).astype(BF16)
    low = (values - high.astype(np.float64)).astype(np.float32).astype(BF16)
    return high, low


def window_table():
    total = TAPS * LENGTH
    places = np.arange(total, dtype=np.float64)
    centred = (places - (total - 1) / 2.0) / LENGTH
    taper = 0.5 - 0.5 * np.cos(2.0 * math.pi / total * (places + 0.5))
    shaped = np.sinc(centred) * taper
    shaped = shaped / np.sqrt(np.sum(shaped * shaped))
    return shaped.reshape(TAPS, INNER, LANES).astype(np.float32)


def first_table():
    idx = np.arange(INNER)
    phase = 2.0 * math.pi / INNER * (np.outer(idx, idx) % INNER)
    high, low = split(np.concatenate([np.cos(phase), -np.sin(phase)], axis=0))
    return np.concatenate([high, high, low], axis=1)


def twist_table():
    phase = 2.0 * math.pi / LENGTH * np.outer(np.arange(INNER), np.arange(LANES))
    return np.stack([np.cos(phase), -np.sin(phase)]).astype(np.float32)


def second_table():
    k1 = 2 * np.arange(32)[None, :] + np.arange(2)[:, None]
    phase = 2.0 * math.pi / LANES * (np.arange(LANES)[:, None, None] * k1[None] % LANES)
    cos, sin = np.cos(phase), np.sin(phase)
    from_real = np.stack([cos, -sin], axis=2).reshape(LANES, LANES)
    from_imag = np.stack([sin, cos], axis=2).reshape(LANES, LANES)
    return np.stack(split(np.concatenate([from_real, from_imag], axis=0)))


def dot(left, right):
    return jnp.dot(left, right, preferred_element_type=F32)


def parts_of(value):
    high = value.astype(BF16)
    return high, (value - high.astype(F32)).astype(BF16)


def front_kernel(own, halo, win, first, twist, second, gain, out, wide, flt, inter):
    for i in range(2):
        wide[i, 0:15] = halo[i].astype(F32)
        wide[i, 15:31] = own[i].astype(F32)

    def filter_step(step, carry):
        i = step // 8
        rows = pl.ds(pl.multiple_of((step % 8) * 8, 8), 8)
        taps = [win[p, rows, :] for p in range(TAPS)]
        xs = [wide[i, t, rows, :] for t in range(31)]
        for t in range(16):
            even = taps[0] * xs[t]
            odd = taps[1] * xs[t + 1]
            for p in range(2, TAPS, 2):
                even = even + taps[p] * xs[t + p]
                odd = odd + taps[p + 1] * xs[t + p + 1]
            flt[i, t, rows, :] = even + odd
        return carry

    lax.fori_loop(0, 16, filter_step, 0)

    low_lanes = lax.broadcasted_iota(jnp.int32, (64, LANES), 1) < 64

    def group_step(g, carry):
        columns = []
        for i in range(2):
            for j in range(2):
                high, low = parts_of(flt[i, 2 * g + j])
                columns.append(jnp.concatenate([high, low, high], axis=0))
        stage = dot(first[...], jnp.concatenate(columns, axis=1))
        t_re, t_im = twist[0], twist[1]
        turned = []
        for row in range(4):
            re = stage[:64, row * 128 : row * 128 + 128]
            im = stage[64:, row * 128 : row * 128 + 128]
            turned.append(
                jnp.concatenate([re * t_re - im * t_im, re * t_im + im * t_re], axis=1)
            )
        high, low = parts_of(jnp.concatenate(turned, axis=0))
        spec = dot(high, second[0]) + dot(low, second[0]) + dot(high, second[1])
        for i in range(2):
            flipped = spec[i * 128 : i * 128 + 128].T
            even, odd = flipped[:64], flipped[64:]
            rows = (
                jnp.where(low_lanes, even, pltpu.roll(odd, 64, 1)),
                jnp.where(low_lanes, pltpu.roll(even, 64, 1), odd),
            )
            for j in range(2):
                for part in range(2):
                    place = part * 4 + i * 2 + j
                    inter[pl.ds(place, 32, stride=8), :] = (
                        rows[j][part * 32 : part * 32 + 32] * gain[i]
                    )
        out[g] = inter[0:256].astype(BF16)
        return carry

    lax.fori_loop(0, 8, group_step, 0)


def front(own, halo, gain):
    args = (
        own,
        halo,
        jnp.asarray(window_table()),
        jnp.asarray(first_table()),
        jnp.asarray(twist_table()),
        jnp.asarray(second_table()),
        gain,
    )
    return pl.pallas_call(
        front_kernel,
        out_shape=jax.ShapeDtypeStruct((8, 256, LANES), BF16),
        scratch_shapes=[
            pltpu.VMEM((2, 31, INNER, LANES), F32),
            pltpu.VMEM((2, 16, INNER, LANES), F32),
            pltpu.VMEM((264, LANES), F32),
        ],
        compiler_params=pltpu.CompilerParams(vmem_limit_bytes=58 << 20),
        cost_estimate=pl.CostEstimate(flops=400_000_000, bytes_accessed=3_000_000, transcendentals=0),
        name="front",
    )(*args)


def weight_kernel(base, turn, out, carry):
    @pl.when(pl.program_id(0) == 0)
    def _():
        carry[...] = base[...]

    for block in range(4):
        cols = pl.ds(block * 256, 256)
        re, im = carry[0, :, cols], carry[1, :, cols]
        t_re, t_im = turn[0, :, cols], turn[1, :, cols]
        for c in range(8):
            out[0, c * 32 : c * 32 + 16, cols] = re.astype(BF16)
            out[0, c * 32 + 16 : c * 32 + 32, cols] = im.astype(BF16)
            re, im = re * t_re - im * t_im, re * t_im + im * t_re
        carry[0, :, cols] = re
        carry[1, :, cols] = im


def weights(delays, first_chan, chan_here):
    beams = delays.shape[0]
    rows = jnp.transpose(delays.reshape(beams, 8, 2), (2, 1, 0)).reshape(INPUTS, beams)
    factor = 1.0 + first_chan.astype(F32) / CHANNELS
    phase = 2.0 * math.pi * (rows * factor)
    base = jnp.stack([jnp.cos(phase), -jnp.sin(phase)])
    step = (2.0 * math.pi / CHANNELS) * rows
    turn = jnp.stack([jnp.cos(step), -jnp.sin(step)])
    groups = chan_here // 8
    whole = pl.BlockSpec((2, INPUTS, beams), lambda k: (0, 0, 0))
    return pl.pallas_call(
        weight_kernel,
        grid=(groups,),
        in_specs=[whole, whole],
        out_specs=pl.BlockSpec((1, 256, beams), lambda k: (k, 0, 0)),
        out_shape=jax.ShapeDtypeStruct((groups, 256, beams), BF16),
        scratch_shapes=[pltpu.VMEM((2, INPUTS, beams), F32)],
        compiler_params=pltpu.CompilerParams(vmem_limit_bytes=50 << 20),
        cost_estimate=pl.CostEstimate(flops=20_000_000, bytes_accessed=9_000_000, transcendentals=0),
        name="weights",
    )(base, turn)


def beam_kernel(spec, w, out, wide, flat, lhs):
    step = pl.program_id(0)

    @pl.when(step == 0)
    def _():
        wide[0:2048] = spec[...].astype(F32)

        def turn(q, carry):
            j, four = q // 8, q % 8
            straight, crossed = [], []
            for p in range(4):
                row = (four * 4 + p) * 8 + j
                got = [wide[pl.ds(row + 2 * r, 8, stride=256), :] for r in range(4)]
                straight += [got[0], got[1], -got[2], -got[3]]
                crossed += [got[2], got[3], got[0], got[1]]
            flat[0, q] = jnp.concatenate(straight, axis=0).T
            flat[1, q] = jnp.concatenate(crossed, axis=0).T
            return carry

        lax.fori_loop(0, 16, turn, 0)

    lane = lax.broadcasted_iota(jnp.int32, (8, LANES), 1) // 32
    chan = lax.broadcasted_iota(jnp.int32, (8, LANES), 0)
    bit0, bit1 = chan % 2 == 1, chan // 2 % 2 == 1
    masks = [jnp.where(chan == lane + 4 * half, 1.0, 0.0).astype(F32) for half in range(2)]
    for group in range(2):
        rows = pl.ds(pl.multiple_of(step * 16 + group * 8, 8), 8)
        for v in range(2):
            for q in range(16):
                spread = flat[v, q, rows, :]
                spread = jnp.where(bit0, pltpu.roll(spread, 32, 1), spread)
                spread = jnp.where(bit1, pltpu.roll(spread, 64, 1), spread)
                each = [spread] + [pltpu.roll(spread, 128 - 32 * p, 1) for p in range(1, 4)]
                at = (v * 16 + q) * 32
                for half in range(2):
                    block = jnp.concatenate([e * masks[half] for e in each], axis=0)
                    lhs[group, at : at + 32, half * 128 : half * 128 + 128] = block.astype(BF16)
    for n in range(4):
        cols = pl.ds(n * 256, 256)
        powers = []
        for group in range(2):
            amp = dot(lhs[group], w[group, :, cols])
            amp = amp * amp
            total = (amp[0:256] + amp[256:512]) + (amp[512:768] + amp[768:1024])
            powers.append(total.reshape(32, 8, 256))
        both = jnp.concatenate(powers, axis=1) * (1.0 / INPUTS)
        out[:, 0, :, cols] = both.astype(BF16)


def beams_of(spec, w, chan_here):
    count = w.shape[2]
    return pl.pallas_call(
        beam_kernel,
        grid=(chan_here // 16,),
        in_specs=[
            pl.BlockSpec((2048, LANES), lambda k: (0, 0)),
            pl.BlockSpec((2, 256, count), lambda k: (k, 0, 0)),
        ],
        out_specs=pl.BlockSpec((32, 1, 16, count), lambda k: (0, 0, k, 0)),
        out_shape=jax.ShapeDtypeStruct((32, 1, chan_here, count), BF16),
        scratch_shapes=[
            pltpu.VMEM((2304, LANES), F32),
            pltpu.VMEM((2, 16, LANES, LANES), F32),
            pltpu.VMEM((2, 1024, 256), BF16),
        ],
        compiler_params=pltpu.CompilerParams(vmem_limit_bytes=58 << 20),
        cost_estimate=pl.CostEstimate(flops=9_000_000_000, bytes_accessed=17_000_000, transcendentals=0),
        name="beams",
    )(spec, w)


def per_device(voltages, eq_gain, delays):
    frames = voltages.reshape(2, 16, INNER, LANES)
    halo = shifted(frames[:, 1:], "shard", 1)
    chan_here = CHANNELS // lax.axis_size("shard")
    messages = front(frames, halo, eq_gain.reshape(2, 32, LANES))
    got = lax.all_to_all(
        messages.reshape(256, 8, LANES), ("grp", "shard"), split_axis=0, concat_axis=0, tiled=True
    )
    w = weights(delays, lax.axis_index("shard") * chan_here, chan_here)
    return beams_of(got.reshape(2048, LANES), w, chan_here)


def solution(mesh):
    placed = (P("grp", "shard"), P("grp", None), P())
    return jax.shard_map(
        per_device,
        mesh=mesh,
        in_specs=placed,
        out_specs=P(None, "grp", "shard", None),
        check_vma=False,
    )
```

```python
import math

import jax
import jax.numpy as jnp
import numpy as np
from jax import lax
from jax.experimental import pallas as pl
from jax.experimental.pallas import tpu as pltpu
from jax.sharding import PartitionSpec as P

CHANNELS = 4096
TAPS = 16
INPUTS = 16
LENGTH = 2 * CHANNELS
INNER = 64
LANES = 128
F32 = jnp.float32
BF16 = jnp.bfloat16


def split(values):
    high = values.astype(np.float32).astype(BF16)
    low = (values - high.astype(np.float64)).astype(np.float32).astype(BF16)
    return high, low


def window_table():
    total = TAPS * LENGTH
    places = np.arange(total, dtype=np.float64)
    centred = (places - (total - 1) / 2.0) / LENGTH
    taper = 0.5 - 0.5 * np.cos(2.0 * math.pi / total * (places + 0.5))
    shaped = np.sinc(centred) * taper
    shaped = shaped / np.sqrt(np.sum(shaped * shaped))
    return shaped.reshape(TAPS, INNER, LANES).astype(np.float32)


def first_table():
    idx = np.arange(INNER)
    phase = 2.0 * math.pi / INNER * (np.outer(idx, idx) % INNER)
    high, low = split(np.concatenate([np.cos(phase), -np.sin(phase)], axis=0))
    return np.concatenate([high, high, low], axis=1)


def twist_table():
    phase = 2.0 * math.pi / LENGTH * np.outer(np.arange(INNER), np.arange(LANES))
    return np.stack([np.cos(phase), -np.sin(phase)]).astype(np.float32)


def second_table():
    k1 = 2 * np.arange(32)[None, :] + np.arange(2)[:, None]
    phase = 2.0 * math.pi / LANES * (np.arange(LANES)[:, None, None] * k1[None] % LANES)
    cos, sin = np.cos(phase), np.sin(phase)
    from_real = np.stack([cos, -sin], axis=2).reshape(LANES, LANES)
    from_imag = np.stack([sin, cos], axis=2).reshape(LANES, LANES)
    return np.stack(split(np.concatenate([from_real, from_imag], axis=0)))


def dot(left, right):
    return jnp.dot(left, right, preferred_element_type=F32)


def parts_of(value):
    high = value.astype(BF16)
    return high, (value - high.astype(F32)).astype(BF16)


def summed(terms):
    lanes = [terms[0], terms[1]] if len(terms) > 1 else [terms[0]]
    for at, term in enumerate(terms[2:]):
        lanes[at % 2] = lanes[at % 2] + term
    return lanes[0] + lanes[1] if len(lanes) > 1 else lanes[0]


def front_kernel(
    keep, before, own, after, win_far, first_far, twist_far, second_far, gain, out,
    wide, flt, inter, win, first, twist, second, arrived,
):
    tables = ((win_far, win), (first_far, first), (twist_far, twist), (second_far, second))
    copies = [
        pltpu.make_async_copy(far, near, arrived.at[at]) for at, (far, near) in enumerate(tables)
    ]
    for copy in copies:
        copy.start()
    for i in range(2):
        wide[i, 0:7] = before[i].astype(F32)
        wide[i, 7:23] = own[i].astype(F32)
        wide[i, 23:31] = after[i].astype(F32)
    keep_old = keep[0]
    for copy in copies:
        copy.wait()

    def filter_step(step, carry):
        i = step // 8
        rows = pl.ds(pl.multiple_of((step % 8) * 8, 8), 8)
        taps = [win[p, rows, :] for p in range(TAPS)]
        xs = [wide[i, t, rows, :] for t in range(31)]
        for t in range(16):
            terms = [taps[p] * xs[t + p] for p in range(TAPS)]
            cut = 23 - t
            if cut >= TAPS:
                total = summed(terms)
            else:
                total = summed(terms[:cut]) * keep_old + summed(terms[cut:])
            flt[i, t, rows, :] = total
        return carry

    lax.fori_loop(0, 16, filter_step, 0)

    low_lanes = lax.broadcasted_iota(jnp.int32, (64, LANES), 1) < 64

    def group_step(g, carry):
        columns = []
        for i in range(2):
            for j in range(2):
                high, low = parts_of(flt[i, 2 * g + j])
                columns.append(jnp.concatenate([high, low, high], axis=0))
        stage = dot(first[...], jnp.concatenate(columns, axis=1))
        t_re, t_im = twist[0], twist[1]
        turned = []
        for row in range(4):
            re = stage[:64, row * 128 : row * 128 + 128]
            im = stage[64:, row * 128 : row * 128 + 128]
            turned.append(
                jnp.concatenate([re * t_re - im * t_im, re * t_im + im * t_re], axis=1)
            )
        high, low = parts_of(jnp.concatenate(turned, axis=0))
        spec = dot(high, second[0]) + dot(low, second[0]) + dot(high, second[1])
        for i in range(2):
            flipped = spec[i * 128 : i * 128 + 128].T
            even, odd = flipped[:64], flipped[64:]
            rows = (
                jnp.where(low_lanes, even, pltpu.roll(odd, 64, 1)),
                jnp.where(low_lanes, pltpu.roll(even, 64, 1), odd),
            )
            for j in range(2):
                for part in range(2):
                    place = part * 4 + i * 2 + j
                    inter[g, pl.ds(place, 32, stride=8), :] = (
                        rows[j][part * 32 : part * 32 + 32] * gain[i]
                    )
        out[(g + 4) % 8] = inter[g, 0:256].astype(BF16)
        return carry

    for g in range(8):
        group_step(g, 0)


def far(table):
    return pltpu.with_memory_space_constraint(jnp.asarray(table), pltpu.HBM)


def front(keep, before, own, after, gain):
    args = (
        keep,
        before,
        own,
        after,
        far(window_table()),
        far(first_table()),
        far(twist_table()),
        far(second_table()),
        gain,
    )
    return pl.pallas_call(
        front_kernel,
        in_specs=[pl.BlockSpec(memory_space=pltpu.SMEM)]
        + [pl.BlockSpec(memory_space=pltpu.VMEM)] * 3
        + [pl.BlockSpec(memory_space=pltpu.HBM)] * 4
        + [pl.BlockSpec(memory_space=pltpu.VMEM)],
        out_shape=jax.ShapeDtypeStruct((8, 256, LANES), BF16),
        scratch_shapes=[
            pltpu.VMEM((2, 31, INNER, LANES), F32),
            pltpu.VMEM((2, 16, INNER, LANES), F32),
            pltpu.VMEM((8, 264, LANES), F32),
            pltpu.VMEM((TAPS, INNER, LANES), F32),
            pltpu.VMEM((128, 192), BF16),
            pltpu.VMEM((2, INNER, LANES), F32),
            pltpu.VMEM((2, 256, LANES), BF16),
            pltpu.SemaphoreType.DMA((4,)),
        ],
        compiler_params=pltpu.CompilerParams(vmem_limit_bytes=24 << 20),
        cost_estimate=pl.CostEstimate(flops=400_000_000, bytes_accessed=3_000_000, transcendentals=0),
        name="front",
    )(*args)


def weight_kernel(base, turn, out, carry):
    @pl.when(pl.program_id(0) == 0)
    def _():
        carry[...] = base[...]

    for block in range(4):
        cols = pl.ds(block * 256, 256)
        re, im = carry[0, :, cols], carry[1, :, cols]
        t_re, t_im = turn[0, :, cols], turn[1, :, cols]
        for c in range(16):
            half, at = c // 8, c % 8 * 32
            out[half, at : at + 16, cols] = re.astype(BF16)
            out[half, at + 16 : at + 32, cols] = im.astype(BF16)
            re, im = re * t_re - im * t_im, re * t_im + im * t_re
        carry[0, :, cols] = re
        carry[1, :, cols] = im


def angles(delays, first_chan):
    beams = delays.shape[0]
    rows = jnp.transpose(delays.reshape(beams, 8, 2), (2, 1, 0)).reshape(INPUTS, beams)
    factor = 1.0 + first_chan.astype(F32) / CHANNELS
    phase = 2.0 * math.pi * (rows * factor)
    base = jnp.stack([jnp.cos(phase), -jnp.sin(phase)])
    step = (2.0 * math.pi / CHANNELS) * rows
    turn = jnp.stack([jnp.cos(step), -jnp.sin(step)])
    return base, turn


def weights(base, turn, chan_here):
    beams = base.shape[2]
    groups = chan_here // 8
    whole = pl.BlockSpec((2, INPUTS, beams), lambda k: (0, 0, 0))
    return pl.pallas_call(
        weight_kernel,
        grid=(groups // 2,),
        in_specs=[whole, whole],
        out_specs=pl.BlockSpec((2, 256, beams), lambda k: (k, 0, 0)),
        out_shape=jax.ShapeDtypeStruct((groups, 256, beams), BF16),
        scratch_shapes=[pltpu.VMEM((2, INPUTS, beams), F32)],
        compiler_params=pltpu.CompilerParams(vmem_limit_bytes=54 << 20),
        cost_estimate=pl.CostEstimate(flops=20_000_000, bytes_accessed=9_000_000, transcendentals=0),
        name="weights",
    )(base, turn)


def beam_kernel(lag, spec, w, out, wide, flat, left, right):
    step = pl.program_id(0)
    lane = lax.broadcasted_iota(jnp.int32, (8, LANES), 1) // 32
    chan = lax.broadcasted_iota(jnp.int32, (8, LANES), 0)
    bit0, bit1 = chan % 2 == 1, chan // 2 % 2 == 1
    masks = [jnp.where(chan == lane + 4 * half, 1.0, 0.0).astype(F32) for half in range(2)]

    def spread_out(first_chan, lhs):
        rows = pl.ds(pl.multiple_of(first_chan, 8), 8)
        for four in range(8):
            for v in range(2):
                shifts = []
                for j in range(2):
                    spread = flat[v, j * 8 + four, rows, :]
                    spread = jnp.where(bit0, pltpu.roll(spread, 32, 1), spread)
                    spread = jnp.where(bit1, pltpu.roll(spread, 64, 1), spread)
                    shifts.append(
                        [spread] + [pltpu.roll(spread, 128 - 32 * p, 1) for p in range(1, 4)]
                    )
                for p in range(4):
                    at = (four * 4 + p) * 32 + v * 16
                    for half in range(2):
                        block = jnp.concatenate([shifts[j][p] * masks[half] for j in range(2)], axis=0)
                        lhs[at : at + 16, half * 128 : half * 128 + 128] = block.astype(BF16)

    @pl.when(step == 0)
    def _():
        wide[0:2048] = spec[...].astype(F32)

        def turn(q, carry):
            j, four = q // 8, q % 8
            straight, crossed = [], []
            for p in range(4):
                row = lax.rem(four * 4 + p + 32 - lag[0], 32) * 8 + j
                got = [wide[pl.ds(row + 2 * r, 8, stride=256), :] for r in range(4)]
                straight += [got[0], got[1], -got[2], -got[3]]
                crossed += [got[2], got[3], got[0], got[1]]
            flat[0, q] = jnp.concatenate(straight, axis=0).T
            flat[1, q] = jnp.concatenate(crossed, axis=0).T
            return carry

        lax.fori_loop(0, 16, turn, 0, unroll=4)
    for group in range(2):
        spread_out(step * 16 + group * 8, (left, right)[group])
    for n in range(4):
        cols = pl.ds(n * 256, 256)
        powers = []
        for group in range(2):
            amp = dot((left, right)[group][...], w[group, :, cols])
            powers.append(jnp.sum((amp * amp).reshape(32, 4, 8, 256), axis=1))
        both = jnp.concatenate(powers, axis=1) * (1.0 / INPUTS)
        out[:, 0, :, cols] = both.astype(BF16)


def beams_of(lag, spec, w, chan_here):
    count = w.shape[2]
    return pl.pallas_call(
        beam_kernel,
        grid=(chan_here // 16,),
        in_specs=[
            pl.BlockSpec(memory_space=pltpu.SMEM),
            pl.BlockSpec(memory_space=pltpu.VMEM),
            pl.BlockSpec((2, 256, count), lambda k: (k, 0, 0)),
        ],
        out_specs=pl.BlockSpec((32, 1, 16, count), lambda k: (0, 0, k, 0)),
        out_shape=jax.ShapeDtypeStruct((32, 1, chan_here, count), BF16),
        scratch_shapes=[
            pltpu.VMEM((2304, LANES), F32),
            pltpu.VMEM((2, 16, LANES, LANES), F32),
            pltpu.VMEM((1024, 256), BF16),
            pltpu.VMEM((1024, 256), BF16),
        ],
        compiler_params=pltpu.CompilerParams(vmem_limit_bytes=40 << 20),
        cost_estimate=pl.CostEstimate(flops=9_000_000_000, bytes_accessed=17_000_000, transcendentals=0),
        name="beams",
    )(lag, spec, w)


def per_device(voltages, eq_gain, delays):
    frames = voltages.reshape(2, 16, INNER, LANES)
    count = lax.axis_size("shard")
    shard = lax.axis_index("shard")
    before = lax.ppermute(frames[:, 9:], "shard", [(at, at + 1) for at in range(count - 1)])
    after = lax.ppermute(frames[:, :8], "shard", [(at, (at - 1) % count) for at in range(count)])
    keep = jnp.where(shard == count - 1, 0.0, 1.0).astype(F32).reshape(1)
    chan_here = CHANNELS // count
    base, turn, gain = lax.optimization_barrier(
        (*angles(delays, shard * chan_here), eq_gain.reshape(2, 32, LANES))
    )
    messages = front(keep, before, frames, after, gain)
    got = lax.all_to_all(
        messages.reshape(256, 8, LANES), ("grp", "shard"), split_axis=0, concat_axis=0, tiled=True
    )
    w = pltpu.with_memory_space_constraint(weights(base, turn, chan_here), pltpu.HBM)
    lag = jnp.where(lax.axis_index("grp") < 4, 1, 0).astype(jnp.int32).reshape(1)
    return beams_of(lag, got.reshape(2048, LANES), w, chan_here)


def solution(mesh):
    placed = (P("grp", "shard"), P("grp", None), P())
    return jax.shard_map(
        per_device,
        mesh=mesh,
        in_specs=placed,
        out_specs=P(None, "grp", "shard", None),
        check_vma=False,
    )
```

```python
import math

import jax
import jax.numpy as jnp
import numpy as np
from jax import lax
from jax.experimental import pallas as pl
from jax.experimental.pallas import tpu as pltpu
from jax.sharding import PartitionSpec as P

CHANNELS = 4096
TAPS = 16
INPUTS = 16
LENGTH = 2 * CHANNELS
INNER = 64
LANES = 128
F32 = jnp.float32
BF16 = jnp.bfloat16


def split(values):
    high = values.astype(np.float32).astype(BF16)
    low = (values - high.astype(np.float64)).astype(np.float32).astype(BF16)
    return high, low


def window_table():
    total = TAPS * LENGTH
    places = np.arange(total, dtype=np.float64)
    centred = (places - (total - 1) / 2.0) / LENGTH
    taper = 0.5 - 0.5 * np.cos(2.0 * math.pi / total * (places + 0.5))
    shaped = np.sinc(centred) * taper
    shaped = shaped / np.sqrt(np.sum(shaped * shaped))
    return shaped.reshape(TAPS, INNER, LANES).astype(np.float32)


def first_table():
    idx = np.arange(INNER)
    phase = 2.0 * math.pi / INNER * (np.outer(idx, idx) % INNER)
    high, low = split(np.concatenate([np.cos(phase), -np.sin(phase)], axis=0))
    return np.concatenate([high, high, low], axis=1)


def twist_table():
    phase = 2.0 * math.pi / LENGTH * np.outer(np.arange(INNER), np.arange(LANES))
    return np.stack([np.cos(phase), -np.sin(phase)]).astype(np.float32)


def second_table():
    k1 = 2 * np.arange(32)[None, :] + np.arange(2)[:, None]
    phase = 2.0 * math.pi / LANES * (np.arange(LANES)[:, None, None] * k1[None] % LANES)
    cos, sin = np.cos(phase), np.sin(phase)
    from_real = np.stack([cos, -sin], axis=2).reshape(LANES, LANES)
    from_imag = np.stack([sin, cos], axis=2).reshape(LANES, LANES)
    return split(np.concatenate([from_real, from_imag], axis=0))[0]


def dot(left, right):
    return jnp.dot(left, right, preferred_element_type=F32)


def parts_of(value):
    high = value.astype(BF16)
    return high, (value - high.astype(F32)).astype(BF16)


def summed(terms):
    lanes = [terms[0], terms[1]] if len(terms) > 1 else [terms[0]]
    for at, term in enumerate(terms[2:]):
        lanes[at % 2] = lanes[at % 2] + term
    return lanes[0] + lanes[1] if len(lanes) > 1 else lanes[0]


def front_kernel(
    keep, before, own, after, win_far, first_far, twist_far, second_far, gain, out,
    wide, flt, inter, win, first, twist, second, arrived,
):
    tables = ((win_far, win), (first_far, first), (twist_far, twist), (second_far, second))
    copies = [
        pltpu.make_async_copy(far, near, arrived.at[at]) for at, (far, near) in enumerate(tables)
    ]
    for copy in copies:
        copy.start()
    for i in range(2):
        wide[i, 0:7] = before[i].astype(F32)
        wide[i, 7:23] = own[i].astype(F32)
        wide[i, 23:31] = after[i].astype(F32)
    keep_old = keep[0]
    for copy in copies:
        copy.wait()

    def filter_step(step, carry):
        i = step // 8
        rows = pl.ds(pl.multiple_of((step % 8) * 8, 8), 8)
        taps = [win[p, rows, :] for p in range(TAPS)]
        xs = [wide[i, t, rows, :] for t in range(31)]
        for t in range(16):
            terms = [taps[p] * xs[t + p] for p in range(TAPS)]
            cut = 23 - t
            if cut >= TAPS:
                total = summed(terms)
            else:
                total = summed(terms[:cut]) * keep_old + summed(terms[cut:])
            flt[i, t, rows, :] = total
        return carry

    lax.fori_loop(0, 16, filter_step, 0)

    low_lanes = lax.broadcasted_iota(jnp.int32, (64, LANES), 1) < 64

    def group_step(g, carry):
        columns = []
        for i in range(2):
            for j in range(2):
                high, low = parts_of(flt[i, 2 * g + j])
                columns.append(jnp.concatenate([high, low, high], axis=0))
        stage = dot(first[...], jnp.concatenate(columns, axis=1))
        t_re, t_im = twist[0], twist[1]
        turned = []
        for row in range(4):
            re = stage[:64, row * 128 : row * 128 + 128]
            im = stage[64:, row * 128 : row * 128 + 128]
            turned.append(
                jnp.concatenate([re * t_re - im * t_im, re * t_im + im * t_re], axis=1)
            )
        spec = dot(jnp.concatenate(turned, axis=0).astype(BF16), second[...])
        for i in range(2):
            flipped = spec[i * 128 : i * 128 + 128].T
            even, odd = flipped[:64], flipped[64:]
            rows = (
                jnp.where(low_lanes, even, pltpu.roll(odd, 64, 1)),
                jnp.where(low_lanes, pltpu.roll(even, 64, 1), odd),
            )
            for j in range(2):
                for part in range(2):
                    place = part * 4 + i * 2 + j
                    inter[g, pl.ds(place, 32, stride=8), :] = (
                        rows[j][part * 32 : part * 32 + 32] * gain[i]
                    )
        out[(g + 4) % 8] = inter[g, 0:256].astype(BF16)
        return carry

    for g in range(8):
        group_step(g, 0)


def far(table):
    return pltpu.with_memory_space_constraint(jnp.asarray(table), pltpu.HBM)


def front(keep, before, own, after, gain):
    args = (
        keep,
        before,
        own,
        after,
        far(window_table()),
        far(first_table()),
        far(twist_table()),
        far(second_table()),
        gain,
    )
    return pl.pallas_call(
        front_kernel,
        in_specs=[pl.BlockSpec(memory_space=pltpu.SMEM)]
        + [pl.BlockSpec(memory_space=pltpu.VMEM)] * 3
        + [pl.BlockSpec(memory_space=pltpu.HBM)] * 4
        + [pl.BlockSpec(memory_space=pltpu.VMEM)],
        out_shape=jax.ShapeDtypeStruct((8, 256, LANES), BF16),
        scratch_shapes=[
            pltpu.VMEM((2, 31, INNER, LANES), F32),
            pltpu.VMEM((2, 16, INNER, LANES), F32),
            pltpu.VMEM((8, 264, LANES), F32),
            pltpu.VMEM((TAPS, INNER, LANES), F32),
            pltpu.VMEM((128, 192), BF16),
            pltpu.VMEM((2, INNER, LANES), F32),
            pltpu.VMEM((256, LANES), BF16),
            pltpu.SemaphoreType.DMA((4,)),
        ],
        compiler_params=pltpu.CompilerParams(vmem_limit_bytes=24 << 20),
        cost_estimate=pl.CostEstimate(flops=400_000_000, bytes_accessed=3_000_000, transcendentals=0),
        name="front",
    )(*args)


def weight_kernel(base, turn, out, carry):
    @pl.when(pl.program_id(0) == 0)
    def _():
        carry[...] = base[...]

    for block in range(4):
        cols = pl.ds(block * 256, 256)
        re, im = carry[0, :, cols], carry[1, :, cols]
        t_re, t_im = turn[0, :, cols], turn[1, :, cols]
        for c in range(16):
            half, at = c // 8, c % 8 * 32
            out[half, at : at + 16, cols] = re.astype(BF16)
            out[half, at + 16 : at + 32, cols] = im.astype(BF16)
            re, im = re * t_re - im * t_im, re * t_im + im * t_re
        carry[0, :, cols] = re
        carry[1, :, cols] = im


def angles(delays, first_chan):
    beams = delays.shape[0]
    rows = jnp.transpose(delays.reshape(beams, 8, 2), (2, 1, 0)).reshape(INPUTS, beams)
    factor = 1.0 + first_chan.astype(F32) / CHANNELS
    phase = 2.0 * math.pi * (rows * factor)
    base = jnp.stack([jnp.cos(phase), -jnp.sin(phase)])
    step = (2.0 * math.pi / CHANNELS) * rows
    turn = jnp.stack([jnp.cos(step), -jnp.sin(step)])
    return base, turn


def weights(base, turn, chan_here):
    beams = base.shape[2]
    groups = chan_here // 8
    whole = pl.BlockSpec((2, INPUTS, beams), lambda k: (0, 0, 0))
    return pl.pallas_call(
        weight_kernel,
        grid=(groups // 2,),
        in_specs=[whole, whole],
        out_specs=pl.BlockSpec((2, 256, beams), lambda k: (k, 0, 0)),
        out_shape=jax.ShapeDtypeStruct((groups, 256, beams), BF16),
        scratch_shapes=[pltpu.VMEM((2, INPUTS, beams), F32)],
        compiler_params=pltpu.CompilerParams(vmem_limit_bytes=54 << 20),
        cost_estimate=pl.CostEstimate(flops=20_000_000, bytes_accessed=9_000_000, transcendentals=0),
        name="weights",
    )(base, turn)


def beam_kernel(lag, spec, w, out, wide, flat, left, right, l2, l3):
    step = pl.program_id(0)
    lane = lax.broadcasted_iota(jnp.int32, (8, LANES), 1) // 32
    chan = lax.broadcasted_iota(jnp.int32, (8, LANES), 0)
    bit0, bit1 = chan % 2 == 1, chan // 2 % 2 == 1
    masks = [jnp.where(chan == lane + 4 * half, 1.0, 0.0).astype(F32) for half in range(2)]

    def spread_out(first_chan, lhs):
        rows = pl.ds(pl.multiple_of(first_chan, 8), 8)
        for four in range(8):
            for v in range(2):
                shifts = []
                for j in range(2):
                    spread = flat[v, j * 8 + four, rows, :]
                    spread = jnp.where(bit0, pltpu.roll(spread, 32, 1), spread)
                    spread = jnp.where(bit1, pltpu.roll(spread, 64, 1), spread)
                    shifts.append(
                        [spread] + [pltpu.roll(spread, 128 - 32 * p, 1) for p in range(1, 4)]
                    )
                for p in range(4):
                    at = (four * 4 + p) * 32 + v * 16
                    for half in range(2):
                        block = jnp.concatenate([shifts[j][p] * masks[half] for j in range(2)], axis=0)
                        lhs[at : at + 16, half * 128 : half * 128 + 128] = block.astype(BF16)

    @pl.when(step == 0)
    def _():
        wide[0:2048] = spec[...].astype(F32)

        def turn(q, carry):
            j, four = q // 8, q % 8
            straight, crossed = [], []
            for p in range(4):
                row = lax.rem(four * 4 + p + 32 - lag[0], 32) * 8 + j
                got = [wide[pl.ds(row + 2 * r, 8, stride=256), :] for r in range(4)]
                straight += [got[0], got[1], -got[2], -got[3]]
                crossed += [got[2], got[3], got[0], got[1]]
            flat[0, q] = jnp.concatenate(straight, axis=0).T
            flat[1, q] = jnp.concatenate(crossed, axis=0).T
            return carry

        lax.fori_loop(0, 16, turn, 0, unroll=16)
    def form(pair, refs):
        for n in range(4):
            cols = pl.ds(n * 256, 256)
            powers = []
            for group in range(2):
                amp = dot(refs[group][...], w[pair * 2 + group, :, cols])
                powers.append(jnp.sum((amp * amp).reshape(32, 4, 8, 256), axis=1))
            both = jnp.concatenate(powers, axis=1) * (1.0 / INPUTS)
            out[:, 0, pair * 16 : pair * 16 + 16, cols] = both.astype(BF16)

    spread_out(step * 32 + 0, left)
    spread_out(step * 32 + 8, right)
    form(0, (left, right))
    spread_out(step * 32 + 16, l2)
    spread_out(step * 32 + 24, l3)
    form(1, (l2, l3))


def beams_of(lag, spec, w, chan_here):
    count = w.shape[2]
    return pl.pallas_call(
        beam_kernel,
        grid=(chan_here // 32,),
        in_specs=[
            pl.BlockSpec(memory_space=pltpu.SMEM),
            pl.BlockSpec(memory_space=pltpu.VMEM),
            pl.BlockSpec((4, 256, count), lambda k: (k, 0, 0)),
        ],
        out_specs=pl.BlockSpec((32, 1, 32, count), lambda k: (0, 0, k, 0)),
        out_shape=jax.ShapeDtypeStruct((32, 1, chan_here, count), BF16),
        scratch_shapes=[
            pltpu.VMEM((2304, LANES), F32),
            pltpu.VMEM((2, 16, LANES, LANES), F32),
            pltpu.VMEM((1024, 256), BF16),
            pltpu.VMEM((1024, 256), BF16),
            pltpu.VMEM((1024, 256), BF16),
            pltpu.VMEM((1024, 256), BF16),
        ],
        compiler_params=pltpu.CompilerParams(vmem_limit_bytes=40 << 20),
        cost_estimate=pl.CostEstimate(flops=9_000_000_000, bytes_accessed=17_000_000, transcendentals=0),
        name="beams",
    )(lag, spec, w)


def per_device(voltages, eq_gain, delays):
    frames = voltages.reshape(2, 16, INNER, LANES)
    count = lax.axis_size("shard")
    shard = lax.axis_index("shard")
    before = lax.ppermute(frames[:, 9:], "shard", [(at, at + 1) for at in range(count - 1)])
    after = lax.ppermute(frames[:, :8], "shard", [(at, (at - 1) % count) for at in range(count)])
    keep = jnp.where(shard == count - 1, 0.0, 1.0).astype(F32).reshape(1)
    chan_here = CHANNELS // count
    base, turn, gain = lax.optimization_barrier(
        (*angles(delays, shard * chan_here), eq_gain.reshape(2, 32, LANES))
    )
    messages = front(keep, before, frames, after, gain)
    got = lax.all_to_all(
        messages.reshape(256, 8, LANES), ("grp", "shard"), split_axis=0, concat_axis=0, tiled=True
    )
    w = pltpu.with_memory_space_constraint(weights(base, turn, chan_here), pltpu.HBM)
    lag = jnp.where(lax.axis_index("grp") < 4, 1, 0).astype(jnp.int32).reshape(1)
    return beams_of(lag, got.reshape(2048, LANES), w, chan_here)


def solution(mesh):
    placed = (P("grp", "shard"), P("grp", None), P())
    return jax.shard_map(
        per_device,
        mesh=mesh,
        in_specs=placed,
        out_specs=P(None, "grp", "shard", None),
        check_vma=False,
    )
```

```python
import math

import jax
import jax.numpy as jnp
import numpy as np
from jax import lax
from jax.experimental import pallas as pl
from jax.experimental.pallas import tpu as pltpu
from jax.sharding import PartitionSpec as P

CHANNELS = 4096
TAPS = 16
INPUTS = 16
LENGTH = 2 * CHANNELS
INNER = 64
LANES = 128
F32 = jnp.float32
BF16 = jnp.bfloat16


def split(values):
    high = values.astype(np.float32).astype(BF16)
    low = (values - high.astype(np.float64)).astype(np.float32).astype(BF16)
    return high, low


def window_table():
    total = TAPS * LENGTH
    places = np.arange(total, dtype=np.float64)
    centred = (places - (total - 1) / 2.0) / LENGTH
    taper = 0.5 - 0.5 * np.cos(2.0 * math.pi / total * (places + 0.5))
    shaped = np.sinc(centred) * taper
    shaped = shaped / np.sqrt(np.sum(shaped * shaped))
    return shaped.reshape(TAPS, INNER, LANES).astype(np.float32)


def first_table():
    idx = np.arange(INNER)
    phase = 2.0 * math.pi / INNER * (np.outer(idx, idx) % INNER)
    high, low = split(np.concatenate([np.cos(phase), -np.sin(phase)], axis=0))
    return np.concatenate([high, high, low], axis=1)


def twist_table():
    phase = 2.0 * math.pi / LENGTH * np.outer(np.arange(INNER), np.arange(LANES))
    return np.stack([np.cos(phase), -np.sin(phase)]).astype(np.float32)


def second_table():
    k1 = 2 * np.arange(32)[None, :] + np.arange(2)[:, None]
    phase = 2.0 * math.pi / LANES * (np.arange(LANES)[:, None, None] * k1[None] % LANES)
    cos, sin = np.cos(phase), np.sin(phase)
    from_real = np.stack([cos, -sin], axis=2).reshape(LANES, LANES)
    from_imag = np.stack([sin, cos], axis=2).reshape(LANES, LANES)
    return split(np.concatenate([from_real, from_imag], axis=0))[0]


def dot(left, right):
    return jnp.dot(left, right, preferred_element_type=F32)


def parts_of(value):
    high = value.astype(BF16)
    return high, (value - high.astype(F32)).astype(BF16)


def summed(terms):
    lanes = [terms[0], terms[1]] if len(terms) > 1 else [terms[0]]
    for at, term in enumerate(terms[2:]):
        lanes[at % 2] = lanes[at % 2] + term
    return lanes[0] + lanes[1] if len(lanes) > 1 else lanes[0]


def front_kernel(
    place, keep, far_side, own, near_side, win_far, first_far, twist_far, second_far, gain, out,
    wide, flt, inter, win, first, twist, second, arrived,
):
    tables = ((win_far, win), (first_far, first), (twist_far, twist), (second_far, second))
    copies = [
        pltpu.make_async_copy(far, near, arrived.at[at]) for at, (far, near) in enumerate(tables)
    ]
    for copy in copies:
        copy.start()
    for i in range(2):
        wide[i, 7:23] = own[i].astype(F32)

    @pl.when(place[0] == 0)
    def _():
        for i in range(2):
            wide[i, 0:7] = far_side[i, 1:8].astype(F32)
            wide[i, 23:31] = near_side[i].astype(F32)

    @pl.when(place[0] != 0)
    def _():
        for i in range(2):
            wide[i, 0:7] = near_side[i, 1:8].astype(F32)
            wide[i, 23:31] = far_side[i].astype(F32)

    keep_old = keep[0]
    for copy in copies:
        copy.wait()

    def filter_step(step, carry):
        i = step // 8
        rows = pl.ds(pl.multiple_of((step % 8) * 8, 8), 8)
        taps = [win[p, rows, :] for p in range(TAPS)]
        xs = [wide[i, t, rows, :] for t in range(31)]
        for t in range(16):
            terms = [taps[p] * xs[t + p] for p in range(TAPS)]
            cut = 23 - t
            if cut >= TAPS:
                total = summed(terms)
            else:
                total = summed(terms[:cut]) * keep_old + summed(terms[cut:])
            flt[i, t, rows, :] = total
        return carry

    lax.fori_loop(0, 16, filter_step, 0)

    low_lanes = lax.broadcasted_iota(jnp.int32, (64, LANES), 1) < 64

    def group_step(g, carry):
        columns = []
        for i in range(2):
            for j in range(2):
                high, low = parts_of(flt[i, 2 * g + j])
                columns.append(jnp.concatenate([high, low, high], axis=0))
        stage = dot(first[...], jnp.concatenate(columns, axis=1))
        t_re, t_im = twist[0], twist[1]
        turned = []
        for row in range(4):
            re = stage[:64, row * 128 : row * 128 + 128]
            im = stage[64:, row * 128 : row * 128 + 128]
            turned.append(
                jnp.concatenate([re * t_re - im * t_im, re * t_im + im * t_re], axis=1)
            )
        spec = dot(jnp.concatenate(turned, axis=0).astype(BF16), second[...])
        for i in range(2):
            flipped = spec[i * 128 : i * 128 + 128].T
            even, odd = flipped[:64], flipped[64:]
            rows = (
                jnp.where(low_lanes, even, pltpu.roll(odd, 64, 1)),
                jnp.where(low_lanes, pltpu.roll(even, 64, 1), odd),
            )
            for j in range(2):
                for part in range(2):
                    place = part * 4 + i * 2 + j
                    inter[g, pl.ds(place, 32, stride=8), :] = (
                        rows[j][part * 32 : part * 32 + 32] * gain[i]
                    )
        out[(g + 4) % 8] = inter[g, 0:256].astype(BF16)
        return carry

    for g in range(8):
        group_step(g, 0)


def far(table):
    return pltpu.with_memory_space_constraint(jnp.asarray(table), pltpu.HBM)


def front(place, keep, far_side, own, near_side, gain):
    args = (
        place,
        keep,
        far_side,
        own,
        near_side,
        far(window_table()),
        far(first_table()),
        far(twist_table()),
        far(second_table()),
        gain,
    )
    return pl.pallas_call(
        front_kernel,
        in_specs=[pl.BlockSpec(memory_space=pltpu.SMEM)] * 2
        + [pl.BlockSpec(memory_space=pltpu.VMEM)] * 3
        + [pl.BlockSpec(memory_space=pltpu.HBM)] * 4
        + [pl.BlockSpec(memory_space=pltpu.VMEM)],
        out_shape=jax.ShapeDtypeStruct((8, 256, LANES), BF16),
        scratch_shapes=[
            pltpu.VMEM((2, 31, INNER, LANES), F32),
            pltpu.VMEM((2, 16, INNER, LANES), F32),
            pltpu.VMEM((8, 264, LANES), F32),
            pltpu.VMEM((TAPS, INNER, LANES), F32),
            pltpu.VMEM((128, 192), BF16),
            pltpu.VMEM((2, INNER, LANES), F32),
            pltpu.VMEM((256, LANES), BF16),
            pltpu.SemaphoreType.DMA((4,)),
        ],
        compiler_params=pltpu.CompilerParams(vmem_limit_bytes=24 << 20),
        cost_estimate=pl.CostEstimate(flops=400_000_000, bytes_accessed=3_000_000, transcendentals=0),
        name="front",
    )(*args)


def weight_kernel(base, turn, out, carry):
    @pl.when(pl.program_id(0) == 0)
    def _():
        carry[...] = base[...]

    for block in range(4):
        cols = pl.ds(block * 256, 256)
        re, im = carry[0, :, cols], carry[1, :, cols]
        t_re, t_im = turn[0, :, cols], turn[1, :, cols]
        for c in range(16):
            half, at = c // 8, c % 8 * 32
            out[half, at : at + 16, cols] = re.astype(BF16)
            out[half, at + 16 : at + 32, cols] = im.astype(BF16)
            re, im = re * t_re - im * t_im, re * t_im + im * t_re
        carry[0, :, cols] = re
        carry[1, :, cols] = im


def angles(delays, first_chan):
    beams = delays.shape[0]
    rows = jnp.transpose(delays.reshape(beams, 8, 2), (2, 1, 0)).reshape(INPUTS, beams)
    factor = 1.0 + first_chan.astype(F32) / CHANNELS
    phase = 2.0 * math.pi * (rows * factor)
    base = jnp.stack([jnp.cos(phase), -jnp.sin(phase)])
    step = (2.0 * math.pi / CHANNELS) * rows
    turn = jnp.stack([jnp.cos(step), -jnp.sin(step)])
    return base, turn


def weights(base, turn, chan_here):
    beams = base.shape[2]
    groups = chan_here // 8
    whole = pl.BlockSpec((2, INPUTS, beams), lambda k: (0, 0, 0))
    return pl.pallas_call(
        weight_kernel,
        grid=(groups // 2,),
        in_specs=[whole, whole],
        out_specs=pl.BlockSpec((2, 256, beams), lambda k: (k, 0, 0)),
        out_shape=jax.ShapeDtypeStruct((groups, 256, beams), BF16),
        scratch_shapes=[pltpu.VMEM((2, INPUTS, beams), F32)],
        compiler_params=pltpu.CompilerParams(vmem_limit_bytes=54 << 20),
        cost_estimate=pl.CostEstimate(flops=20_000_000, bytes_accessed=9_000_000, transcendentals=0),
        name="weights",
    )(base, turn)


def beam_kernel(lag, spec, w, out, wide, flat, left, right, l2, l3):
    step = pl.program_id(0)
    lane = lax.broadcasted_iota(jnp.int32, (8, LANES), 1) // 32
    chan = lax.broadcasted_iota(jnp.int32, (8, LANES), 0)
    bit0, bit1 = chan % 2 == 1, chan // 2 % 2 == 1
    masks = [jnp.where(chan == lane + 4 * half, 1.0, 0.0).astype(F32) for half in range(2)]

    def spread_out(first_chan, lhs):
        rows = pl.ds(pl.multiple_of(first_chan, 8), 8)
        for four in range(8):
            for v in range(2):
                shifts = []
                for j in range(2):
                    spread = flat[v, j * 8 + four, rows, :]
                    spread = jnp.where(bit0, pltpu.roll(spread, 32, 1), spread)
                    spread = jnp.where(bit1, pltpu.roll(spread, 64, 1), spread)
                    shifts.append(
                        [spread] + [pltpu.roll(spread, 128 - 32 * p, 1) for p in range(1, 4)]
                    )
                for p in range(4):
                    at = (four * 4 + p) * 32 + v * 16
                    for half in range(2):
                        block = jnp.concatenate([shifts[j][p] * masks[half] for j in range(2)], axis=0)
                        lhs[at : at + 16, half * 128 : half * 128 + 128] = block.astype(BF16)

    @pl.when(step == 0)
    def _():
        wide[0:2048] = spec[...].astype(F32)

        def turn(q, carry):
            j, four = q // 8, q % 8
            straight, crossed = [], []
            for p in range(4):
                row = lax.rem(four * 4 + p + 32 - lag[0], 32) * 8 + j
                got = [wide[pl.ds(row + 2 * r, 8, stride=256), :] for r in range(4)]
                straight += [got[0], got[1], -got[2], -got[3]]
                crossed += [got[2], got[3], got[0], got[1]]
            flat[0, q] = jnp.concatenate(straight, axis=0).T
            flat[1, q] = jnp.concatenate(crossed, axis=0).T
            return carry

        lax.fori_loop(0, 16, turn, 0, unroll=16)

    def form(pair, refs):
        for n in range(4):
            cols = pl.ds(n * 256, 256)
            powers = []
            for group in range(2):
                amp = dot(refs[group][...], w[pair * 2 + group, :, cols])
                powers.append(jnp.sum((amp * amp).reshape(32, 4, 8, 256), axis=1))
            both = jnp.concatenate(powers, axis=1) * (1.0 / INPUTS)
            out[:, 0, pair * 16 : pair * 16 + 16, cols] = both.astype(BF16)

    spread_out(step * 32, left)
    spread_out(step * 32 + 8, right)
    form(0, (left, right))
    spread_out(step * 32 + 16, l2)
    spread_out(step * 32 + 24, l3)
    form(1, (l2, l3))


def beams_of(lag, spec, w, chan_here):
    count = w.shape[2]
    return pl.pallas_call(
        beam_kernel,
        grid=(chan_here // 32,),
        in_specs=[
            pl.BlockSpec(memory_space=pltpu.SMEM),
            pl.BlockSpec(memory_space=pltpu.VMEM),
            pl.BlockSpec((4, 256, count), lambda k: (k, 0, 0)),
        ],
        out_specs=pl.BlockSpec((32, 1, 32, count), lambda k: (0, 0, k, 0)),
        out_shape=jax.ShapeDtypeStruct((32, 1, chan_here, count), BF16),
        scratch_shapes=[
            pltpu.VMEM((2304, LANES), F32),
            pltpu.VMEM((2, 16, LANES, LANES), F32),
            pltpu.VMEM((1024, 256), BF16),
            pltpu.VMEM((1024, 256), BF16),
            pltpu.VMEM((1024, 256), BF16),
            pltpu.VMEM((1024, 256), BF16),
        ],
        compiler_params=pltpu.CompilerParams(vmem_limit_bytes=40 << 20),
        cost_estimate=pl.CostEstimate(flops=9_000_000_000, bytes_accessed=17_000_000, transcendentals=0),
        name="beams",
    )(lag, spec, w)


def per_device(voltages, eq_gain, delays):
    frames = voltages.reshape(2, 16, INNER, LANES)
    count = lax.axis_size("shard")
    shard = lax.axis_index("shard")
    place = shard % 2
    halves = frames.reshape(2, 2, 8, INNER, LANES)
    outer = lax.dynamic_index_in_dim(halves, place, 1, keepdims=False)
    inner = lax.dynamic_index_in_dim(halves, 1 - place, 1, keepdims=False)
    swaps = [(at, (at - 1) % count) for at in range(0, count, 2)]
    far_side = lax.ppermute(outer, "shard", swaps + [(at, at + 1) for at in range(1, count - 1, 2)])
    near_side = lax.ppermute(inner, "shard", [(at, at ^ 1) for at in range(count)])
    keep = jnp.where(shard == count - 1, 0.0, 1.0).astype(F32).reshape(1)
    chan_here = CHANNELS // count
    base, turn, gain = lax.optimization_barrier(
        (*angles(delays, shard * chan_here), eq_gain.reshape(2, 32, LANES))
    )
    place = place.astype(jnp.int32).reshape(1)
    messages = front(place, keep, far_side, frames, near_side, gain)
    got = lax.all_to_all(
        messages.reshape(256, 8, LANES), ("grp", "shard"), split_axis=0, concat_axis=0, tiled=True
    )
    w = pltpu.with_memory_space_constraint(weights(base, turn, chan_here), pltpu.HBM)
    lag = jnp.where(lax.axis_index("grp") < 4, 1, 0).astype(jnp.int32).reshape(1)
    return beams_of(lag, got.reshape(2048, LANES), w, chan_here)


def solution(mesh):
    placed = (P("grp", "shard"), P("grp", None), P())
    return jax.shard_map(
        per_device,
        mesh=mesh,
        in_specs=placed,
        out_specs=P(None, "grp", "shard", None),
        check_vma=False,
    )
```

```python
import math

import jax
import jax.numpy as jnp
import numpy as np
from jax import lax
from jax.experimental import pallas as pl
from jax.experimental.pallas import tpu as pltpu
from jax.sharding import PartitionSpec as P

CHANNELS = 4096
TAPS = 16
INPUTS = 16
LENGTH = 2 * CHANNELS
INNER = 64
LANES = 128
F32 = jnp.float32
BF16 = jnp.bfloat16


def split(values):
    high = values.astype(np.float32).astype(BF16)
    low = (values - high.astype(np.float64)).astype(np.float32).astype(BF16)
    return high, low


def window_table():
    total = TAPS * LENGTH
    places = np.arange(total, dtype=np.float64)
    centred = (places - (total - 1) / 2.0) / LENGTH
    taper = 0.5 - 0.5 * np.cos(2.0 * math.pi / total * (places + 0.5))
    shaped = np.sinc(centred) * taper
    shaped = shaped / np.sqrt(np.sum(shaped * shaped))
    return shaped.reshape(TAPS, INNER, LANES).astype(np.float32)


def first_table():
    idx = np.arange(INNER)
    phase = 2.0 * math.pi / INNER * (np.outer(idx, idx) % INNER)
    high, low = split(np.concatenate([np.cos(phase), -np.sin(phase)], axis=0))
    return np.concatenate([high, high, low], axis=1)


def twist_table():
    phase = 2.0 * math.pi / LENGTH * np.outer(np.arange(INNER), np.arange(LANES))
    return np.stack([np.cos(phase), -np.sin(phase)]).astype(np.float32)


def second_table():
    k1 = 2 * np.arange(32)[None, :] + np.arange(2)[:, None]
    phase = 2.0 * math.pi / LANES * (np.arange(LANES)[:, None, None] * k1[None] % LANES)
    cos, sin = np.cos(phase), np.sin(phase)
    from_real = np.stack([cos, -sin], axis=2).reshape(LANES, LANES)
    from_imag = np.stack([sin, cos], axis=2).reshape(LANES, LANES)
    return split(np.concatenate([from_real, from_imag], axis=0))[0]


def dot(left, right):
    return jnp.dot(left, right, preferred_element_type=F32)


def parts_of(value):
    high = value.astype(BF16)
    return high, (value - high.astype(F32)).astype(BF16)


def summed(terms):
    lanes = [terms[0], terms[1]] if len(terms) > 1 else [terms[0]]
    for at, term in enumerate(terms[2:]):
        lanes[at % 2] = lanes[at % 2] + term
    return lanes[0] + lanes[1] if len(lanes) > 1 else lanes[0]


def front_kernel(
    place, keep, far_side, own, near_side, win_far, first_far, twist_far, second_far, gain, out,
    wide, flt, inter, win, first, twist, second, arrived, ready, left,
):
    tables = ((win_far, win), (first_far, first), (twist_far, twist), (second_far, second))
    copies = [
        pltpu.make_async_copy(far, near, arrived.at[at]) for at, (far, near) in enumerate(tables)
    ]
    for copy in copies:
        copy.start()
    sends = [
        pltpu.make_async_copy(ready.at[g], out.at[(g + 4) % 8], left.at[g]) for g in range(8)
    ]
    for i in range(2):
        wide[i, 7:23] = own[i].astype(F32)

    @pl.when(place[0] == 0)
    def _():
        for i in range(2):
            wide[i, 0:7] = far_side[i, 1:8].astype(F32)
            wide[i, 23:31] = near_side[i].astype(F32)

    @pl.when(place[0] != 0)
    def _():
        for i in range(2):
            wide[i, 0:7] = near_side[i, 1:8].astype(F32)
            wide[i, 23:31] = far_side[i].astype(F32)

    keep_old = keep[0]
    for copy in copies:
        copy.wait()

    def filter_step(step, carry):
        i = step // 8
        rows = pl.ds(pl.multiple_of((step % 8) * 8, 8), 8)
        taps = [win[p, rows, :] for p in range(TAPS)]
        xs = [wide[i, t, rows, :] for t in range(31)]
        for t in range(16):
            terms = [taps[p] * xs[t + p] for p in range(TAPS)]
            cut = 23 - t
            if cut >= TAPS:
                total = summed(terms)
            else:
                total = summed(terms[:cut]) * keep_old + summed(terms[cut:])
            flt[i, t, rows, :] = total
        return carry

    lax.fori_loop(0, 16, filter_step, 0)

    low_lanes = lax.broadcasted_iota(jnp.int32, (64, LANES), 1) < 64

    def group_step(g, carry):
        columns = []
        for i in range(2):
            for j in range(2):
                high, low = parts_of(flt[i, 2 * g + j])
                columns.append(jnp.concatenate([high, low, high], axis=0))
        stage = dot(first[...], jnp.concatenate(columns, axis=1))
        t_re, t_im = twist[0], twist[1]
        turned = []
        for row in range(4):
            re = stage[:64, row * 128 : row * 128 + 128]
            im = stage[64:, row * 128 : row * 128 + 128]
            turned.append(
                jnp.concatenate([re * t_re - im * t_im, re * t_im + im * t_re], axis=1)
            )
        spec = dot(jnp.concatenate(turned, axis=0).astype(BF16), second[...])
        for i in range(2):
            flipped = spec[i * 128 : i * 128 + 128].T
            even, odd = flipped[:64], flipped[64:]
            rows = (
                jnp.where(low_lanes, even, pltpu.roll(odd, 64, 1)),
                jnp.where(low_lanes, pltpu.roll(even, 64, 1), odd),
            )
            for j in range(2):
                for part in range(2):
                    place = part * 4 + i * 2 + j
                    inter[g, pl.ds(place, 32, stride=8), :] = (
                        rows[j][part * 32 : part * 32 + 32] * gain[i]
                    )
        ready[g] = inter[g, 0:256].astype(BF16)
        sends[g].start()
        return carry

    for g in range(8):
        group_step(g, 0)
    for send in sends:
        send.wait()


def far(table):
    return pltpu.with_memory_space_constraint(jnp.asarray(table), pltpu.HBM)


def front(place, keep, far_side, own, near_side, gain):
    args = (
        place,
        keep,
        far_side,
        own,
        near_side,
        far(window_table()),
        far(first_table()),
        far(twist_table()),
        far(second_table()),
        gain,
    )
    return pl.pallas_call(
        front_kernel,
        in_specs=[pl.BlockSpec(memory_space=pltpu.SMEM)] * 2
        + [pl.BlockSpec(memory_space=pltpu.VMEM)] * 3
        + [pl.BlockSpec(memory_space=pltpu.HBM)] * 4
        + [pl.BlockSpec(memory_space=pltpu.VMEM)],
        out_specs=pl.BlockSpec(memory_space=pltpu.HBM),
        out_shape=jax.ShapeDtypeStruct((8, 256, LANES), BF16),
        scratch_shapes=[
            pltpu.VMEM((2, 31, INNER, LANES), F32),
            pltpu.VMEM((2, 16, INNER, LANES), F32),
            pltpu.VMEM((8, 264, LANES), F32),
            pltpu.VMEM((TAPS, INNER, LANES), F32),
            pltpu.VMEM((128, 192), BF16),
            pltpu.VMEM((2, INNER, LANES), F32),
            pltpu.VMEM((256, LANES), BF16),
            pltpu.SemaphoreType.DMA((4,)),
            pltpu.VMEM((8, 256, LANES), BF16),
            pltpu.SemaphoreType.DMA((8,)),
        ],
        compiler_params=pltpu.CompilerParams(vmem_limit_bytes=24 << 20),
        cost_estimate=pl.CostEstimate(flops=400_000_000, bytes_accessed=3_000_000, transcendentals=0),
        name="front",
    )(*args)


def weight_kernel(base, turn, out, carry):
    @pl.when(pl.program_id(0) == 0)
    def _():
        carry[...] = base[...]

    for block in range(4):
        cols = pl.ds(block * 256, 256)
        re, im = carry[0, :, cols], carry[1, :, cols]
        t_re, t_im = turn[0, :, cols], turn[1, :, cols]
        for c in range(16):
            half, at = c // 8, c % 8 * 32
            out[half, at : at + 16, cols] = re.astype(BF16)
            out[half, at + 16 : at + 32, cols] = im.astype(BF16)
            re, im = re * t_re - im * t_im, re * t_im + im * t_re
        carry[0, :, cols] = re
        carry[1, :, cols] = im


def angles(delays, first_chan):
    beams = delays.shape[0]
    rows = jnp.transpose(delays.reshape(beams, 8, 2), (2, 1, 0)).reshape(INPUTS, beams)
    factor = 1.0 + first_chan.astype(F32) / CHANNELS
    phase = 2.0 * math.pi * (rows * factor)
    base = jnp.stack([jnp.cos(phase), -jnp.sin(phase)])
    step = (2.0 * math.pi / CHANNELS) * rows
    turn = jnp.stack([jnp.cos(step), -jnp.sin(step)])
    return base, turn


def weights(base, turn, chan_here):
    beams = base.shape[2]
    groups = chan_here // 8
    whole = pl.BlockSpec((2, INPUTS, beams), lambda k: (0, 0, 0))
    return pl.pallas_call(
        weight_kernel,
        grid=(groups // 2,),
        in_specs=[whole, whole],
        out_specs=pl.BlockSpec((2, 256, beams), lambda k: (k, 0, 0)),
        out_shape=jax.ShapeDtypeStruct((groups, 256, beams), BF16),
        scratch_shapes=[pltpu.VMEM((2, INPUTS, beams), F32)],
        compiler_params=pltpu.CompilerParams(vmem_limit_bytes=54 << 20),
        cost_estimate=pl.CostEstimate(flops=20_000_000, bytes_accessed=9_000_000, transcendentals=0),
        name="weights",
    )(base, turn)


def beam_kernel(lag, spec, w_far, out, held, arrived, wide, flat, left, right, l2, l3):
    step = pl.program_id(0)
    slot = lax.rem(step, 2)
    w = held.at[slot]

    def fetch(at, into):
        blocks = w_far.at[pl.ds(at * 4, 4)]
        return pltpu.make_async_copy(blocks, held.at[into], arrived.at[into])

    lane = lax.broadcasted_iota(jnp.int32, (8, LANES), 1) // 32
    chan = lax.broadcasted_iota(jnp.int32, (8, LANES), 0)
    bit0, bit1 = chan % 2 == 1, chan // 2 % 2 == 1
    masks = [jnp.where(chan == lane + 4 * half, 1.0, 0.0).astype(F32) for half in range(2)]

    def spread_out(first_chan, lhs):
        rows = pl.ds(pl.multiple_of(first_chan, 8), 8)
        for four in range(8):
            for v in range(2):
                shifts = []
                for j in range(2):
                    spread = flat[v, j * 8 + four, rows, :]
                    spread = jnp.where(bit0, pltpu.roll(spread, 32, 1), spread)
                    spread = jnp.where(bit1, pltpu.roll(spread, 64, 1), spread)
                    shifts.append(
                        [spread] + [pltpu.roll(spread, 128 - 32 * p, 1) for p in range(1, 4)]
                    )
                for p in range(4):
                    at = (four * 4 + p) * 32 + v * 16
                    for half in range(2):
                        block = jnp.concatenate([shifts[j][p] * masks[half] for j in range(2)], axis=0)
                        lhs[at : at + 16, half * 128 : half * 128 + 128] = block.astype(BF16)

    @pl.when(step == 0)
    def _():
        fetch(0, 0).start()
        wide[0:2048] = spec[...].astype(F32)

        def turn(q, carry):
            j, four = q // 8, q % 8
            straight, crossed = [], []
            for p in range(4):
                row = lax.rem(four * 4 + p + 32 - lag[0], 32) * 8 + j
                got = [wide[pl.ds(row + 2 * r, 8, stride=256), :] for r in range(4)]
                straight += [got[0], got[1], -got[2], -got[3]]
                crossed += [got[2], got[3], got[0], got[1]]
            flat[0, q] = jnp.concatenate(straight, axis=0).T
            flat[1, q] = jnp.concatenate(crossed, axis=0).T
            return carry

        lax.fori_loop(0, 16, turn, 0, unroll=16)

    @pl.when(step + 1 < pl.num_programs(0))
    def _():
        fetch(step + 1, 1 - slot).start()

    fetch(step, slot).wait()

    def form(pair, refs):
        for n in range(4):
            cols = pl.ds(n * 256, 256)
            powers = []
            for group in range(2):
                amp = dot(refs[group][...], w[pair * 2 + group, :, cols])
                powers.append(jnp.sum((amp * amp).reshape(32, 4, 8, 256), axis=1))
            both = jnp.concatenate(powers, axis=1) * (1.0 / INPUTS)
            out[:, 0, pair * 16 : pair * 16 + 16, cols] = both.astype(BF16)

    spread_out(step * 32, left)
    spread_out(step * 32 + 8, right)
    form(0, (left, right))
    spread_out(step * 32 + 16, l2)
    spread_out(step * 32 + 24, l3)
    form(1, (l2, l3))


def beams_of(lag, spec, w, chan_here):
    count = w.shape[2]
    return pl.pallas_call(
        beam_kernel,
        grid=(chan_here // 32,),
        in_specs=[
            pl.BlockSpec(memory_space=pltpu.SMEM),
            pl.BlockSpec(memory_space=pltpu.VMEM),
            pl.BlockSpec(memory_space=pltpu.HBM),
        ],
        out_specs=pl.BlockSpec((32, 1, 32, count), lambda k: (0, 0, k, 0)),
        out_shape=jax.ShapeDtypeStruct((32, 1, chan_here, count), BF16),
        scratch_shapes=[
            pltpu.VMEM((2, 4, 256, count), BF16),
            pltpu.SemaphoreType.DMA((2,)),
            pltpu.VMEM((2304, LANES), F32),
            pltpu.VMEM((2, 16, LANES, LANES), F32),
            pltpu.VMEM((1024, 256), BF16),
            pltpu.VMEM((1024, 256), BF16),
            pltpu.VMEM((1024, 256), BF16),
            pltpu.VMEM((1024, 256), BF16),
        ],
        compiler_params=pltpu.CompilerParams(vmem_limit_bytes=40 << 20),
        cost_estimate=pl.CostEstimate(flops=9_000_000_000, bytes_accessed=17_000_000, transcendentals=0),
        name="beams",
    )(lag, spec, w)


def per_device(voltages, eq_gain, delays):
    frames = voltages.reshape(2, 16, INNER, LANES)
    count = lax.axis_size("shard")
    shard = lax.axis_index("shard")
    place = shard % 2
    halves = frames.reshape(2, 2, 8, INNER, LANES)
    outer = lax.dynamic_slice_in_dim(voltages, place * (8 * LENGTH), 8 * LENGTH, 1)
    outer = outer.reshape(2, 8, INNER, LANES)
    inner = lax.dynamic_index_in_dim(halves, 1 - place, 1, keepdims=False)
    swaps = [(at, (at - 1) % count) for at in range(0, count, 2)]
    far_side = lax.ppermute(outer, "shard", swaps + [(at, at + 1) for at in range(1, count - 1, 2)])
    near_side = lax.ppermute(inner, "shard", [(at, at ^ 1) for at in range(count)])
    keep = jnp.where(shard == count - 1, 0.0, 1.0).astype(F32).reshape(1)
    chan_here = CHANNELS // count
    base, turn, gain = lax.optimization_barrier(
        (*angles(delays, shard * chan_here), eq_gain.reshape(2, 32, LANES))
    )
    place = place.astype(jnp.int32).reshape(1)
    messages = front(place, keep, far_side, frames, near_side, gain)
    got = lax.all_to_all(
        messages.reshape(256, 8, LANES), ("grp", "shard"), split_axis=0, concat_axis=0, tiled=True
    )
    w = pltpu.with_memory_space_constraint(weights(base, turn, chan_here), pltpu.HBM)
    lag = jnp.where(lax.axis_index("grp") < 4, 1, 0).astype(jnp.int32).reshape(1)
    return beams_of(lag, got.reshape(2048, LANES), w, chan_here)


def solution(mesh):
    placed = (P("grp", "shard"), P("grp", None), P())
    return jax.shard_map(
        per_device,
        mesh=mesh,
        in_specs=placed,
        out_specs=P(None, "grp", "shard", None),
        check_vma=False,
    )
```

```python
import math

import jax
import jax.numpy as jnp
import numpy as np
from jax import lax
from jax.experimental import pallas as pl
from jax.experimental.pallas import tpu as pltpu
from jax.sharding import PartitionSpec as P

CHANNELS = 4096
TAPS = 16
INPUTS = 16
LENGTH = 2 * CHANNELS
INNER = 64
LANES = 128
F32 = jnp.float32
BF16 = jnp.bfloat16


def split(values):
    high = values.astype(np.float32).astype(BF16)
    low = (values - high.astype(np.float64)).astype(np.float32).astype(BF16)
    return high, low


def window_table():
    total = TAPS * LENGTH
    places = np.arange(total, dtype=np.float64)
    centred = (places - (total - 1) / 2.0) / LENGTH
    taper = 0.5 - 0.5 * np.cos(2.0 * math.pi / total * (places + 0.5))
    shaped = np.sinc(centred) * taper
    shaped = shaped / np.sqrt(np.sum(shaped * shaped))
    return shaped.reshape(TAPS, INNER, LANES).astype(np.float32)


def first_table():
    idx = np.arange(INNER)
    phase = 2.0 * math.pi / INNER * (np.outer(idx, idx) % INNER)
    high, low = split(np.concatenate([np.cos(phase), -np.sin(phase)], axis=0))
    return np.concatenate([high, high, low], axis=1)


def twist_table():
    phase = 2.0 * math.pi / LENGTH * np.outer(np.arange(INNER), np.arange(LANES))
    return np.stack([np.cos(phase), -np.sin(phase)]).astype(np.float32)


def second_table():
    k1 = 2 * np.arange(32)[None, :] + np.arange(2)[:, None]
    phase = 2.0 * math.pi / LANES * (np.arange(LANES)[:, None, None] * k1[None] % LANES)
    cos, sin = np.cos(phase), np.sin(phase)
    from_real = np.stack([cos, -sin], axis=2).reshape(LANES, LANES)
    from_imag = np.stack([sin, cos], axis=2).reshape(LANES, LANES)
    return split(np.concatenate([from_real, from_imag], axis=0))[0]


def dot(left, right):
    return jnp.dot(left, right, preferred_element_type=F32)


def parts_of(value):
    high = value.astype(BF16)
    return high, (value - high.astype(F32)).astype(BF16)


def summed(terms):
    lanes = [terms[0], terms[1]] if len(terms) > 1 else [terms[0]]
    for at, term in enumerate(terms[2:]):
        lanes[at % 2] = lanes[at % 2] + term
    return lanes[0] + lanes[1] if len(lanes) > 1 else lanes[0]


def own_kernel(
    keep, own, win_far, first_far, twist_far, second_far,
    partial, win, first, twist, second, wide, arrived,
):
    tables = ((win_far, win), (first_far, first), (twist_far, twist), (second_far, second))
    copies = [
        pltpu.make_async_copy(far, near, arrived.at[at]) for at, (far, near) in enumerate(tables)
    ]
    for copy in copies:
        copy.start()
    for i in range(2):
        wide[i] = own[i].astype(F32)
    for copy in copies:
        copy.wait()
    keep_old = keep[0]

    def filter_step(step, carry):
        i = step // 8
        rows = pl.ds(pl.multiple_of((step % 8) * 8, 8), 8)
        taps = [win[p, rows, :] for p in range(TAPS)]
        xs = [wide[i, t, rows, :] for t in range(16)]
        for t in range(16):
            total = summed([taps[p] * xs[t + p - 7] for p in range(TAPS) if 7 <= t + p < 23])
            partial[i, t, rows, :] = total * keep_old if t >= 8 else total
        return carry

    lax.fori_loop(0, 16, filter_step, 0)


def far(table):
    return pltpu.with_memory_space_constraint(jnp.asarray(table), pltpu.HBM)


def own_part(keep, own):
    args = (
        keep,
        own,
        far(window_table()),
        far(first_table()),
        far(twist_table()),
        far(second_table()),
    )
    return pl.pallas_call(
        own_kernel,
        in_specs=[
            pl.BlockSpec(memory_space=pltpu.SMEM),
            pl.BlockSpec(memory_space=pltpu.VMEM),
        ]
        + [pl.BlockSpec(memory_space=pltpu.HBM)] * 4,
        out_shape=(
            jax.ShapeDtypeStruct((2, 16, INNER, LANES), F32),
            jax.ShapeDtypeStruct((TAPS, INNER, LANES), F32),
            jax.ShapeDtypeStruct((128, 192), BF16),
            jax.ShapeDtypeStruct((2, INNER, LANES), F32),
            jax.ShapeDtypeStruct((256, LANES), BF16),
        ),
        scratch_shapes=[
            pltpu.VMEM((2, 16, INNER, LANES), F32),
            pltpu.SemaphoreType.DMA((4,)),
        ],
        compiler_params=pltpu.CompilerParams(vmem_limit_bytes=24 << 20),
        cost_estimate=pl.CostEstimate(flops=8_000_000, bytes_accessed=3_000_000, transcendentals=0),
        name="own_part",
    )(*args)


def front_kernel(
    place, far_side, near_side, partial, win, first, twist, second, gain, out,
    wide, flt, inter, ready, left,
):
    sends = [
        pltpu.make_async_copy(ready.at[g], out.at[(g + 4) % 8], left.at[g]) for g in range(8)
    ]

    @pl.when(place[0] == 0)
    def _():
        for i in range(2):
            wide[i, 0:7] = far_side[i, 1:8].astype(F32)
            wide[i, 7:15] = near_side[i].astype(F32)

    @pl.when(place[0] != 0)
    def _():
        for i in range(2):
            wide[i, 0:7] = near_side[i, 1:8].astype(F32)
            wide[i, 7:15] = far_side[i].astype(F32)

    def filter_step(step, carry):
        i = step // 8
        rows = pl.ds(pl.multiple_of((step % 8) * 8, 8), 8)
        taps = [win[p, rows, :] for p in range(TAPS)]
        xs = [wide[i, t, rows, :] for t in range(15)]
        for t in range(16):
            total = partial[i, t, rows, :]
            terms = [taps[p] * xs[t + p] for p in range(TAPS) if t + p < 7]
            terms += [taps[p] * xs[t + p - 16] for p in range(TAPS) if t + p >= 23]
            flt[i, t, rows, :] = total + summed(terms) if terms else total
        return carry

    lax.fori_loop(0, 16, filter_step, 0)

    low_lanes = lax.broadcasted_iota(jnp.int32, (64, LANES), 1) < 64

    def group_step(g, carry):
        columns = []
        for i in range(2):
            for j in range(2):
                high, low = parts_of(flt[i, 2 * g + j])
                columns.append(jnp.concatenate([high, low, high], axis=0))
        stage = dot(first[...], jnp.concatenate(columns, axis=1))
        t_re, t_im = twist[0], twist[1]
        turned = []
        for row in range(4):
            re = stage[:64, row * 128 : row * 128 + 128]
            im = stage[64:, row * 128 : row * 128 + 128]
            turned.append(
                jnp.concatenate([re * t_re - im * t_im, re * t_im + im * t_re], axis=1)
            )
        spec = dot(jnp.concatenate(turned, axis=0).astype(BF16), second[...])
        for i in range(2):
            flipped = spec[i * 128 : i * 128 + 128].T
            even, odd = flipped[:64], flipped[64:]
            rows = (
                jnp.where(low_lanes, even, pltpu.roll(odd, 64, 1)),
                jnp.where(low_lanes, pltpu.roll(even, 64, 1), odd),
            )
            for j in range(2):
                for part in range(2):
                    place = part * 4 + i * 2 + j
                    inter[g, pl.ds(place, 32, stride=8), :] = (
                        rows[j][part * 32 : part * 32 + 32] * gain[i]
                    )
        ready[g] = inter[g, 0:256].astype(BF16)
        sends[g].start()
        return carry

    for g in range(8):
        group_step(g, 0)
    for send in sends:
        send.wait()


def front(place, far_side, near_side, own, gain):
    args = (place, far_side, near_side, *own, gain)
    return pl.pallas_call(
        front_kernel,
        in_specs=[pl.BlockSpec(memory_space=pltpu.SMEM)]
        + [pl.BlockSpec(memory_space=pltpu.VMEM)] * 8,
        out_specs=pl.BlockSpec(memory_space=pltpu.HBM),
        out_shape=jax.ShapeDtypeStruct((8, 256, LANES), BF16),
        scratch_shapes=[
            pltpu.VMEM((2, 15, INNER, LANES), F32),
            pltpu.VMEM((2, 16, INNER, LANES), F32),
            pltpu.VMEM((8, 264, LANES), F32),
            pltpu.VMEM((8, 256, LANES), BF16),
            pltpu.SemaphoreType.DMA((8,)),
        ],
        compiler_params=pltpu.CompilerParams(vmem_limit_bytes=24 << 20),
        cost_estimate=pl.CostEstimate(flops=400_000_000, bytes_accessed=3_000_000, transcendentals=0),
        name="front",
    )(*args)


def weight_kernel(base, turn, out, carry):
    @pl.when(pl.program_id(0) == 0)
    def _():
        carry[...] = base[...]

    for block in range(4):
        cols = pl.ds(block * 256, 256)
        re, im = carry[0, :, cols], carry[1, :, cols]
        t_re, t_im = turn[0, :, cols], turn[1, :, cols]
        for c in range(16):
            half, at = c // 8, c % 8 * 32
            out[half, at : at + 16, cols] = re.astype(BF16)
            out[half, at + 16 : at + 32, cols] = im.astype(BF16)
            re, im = re * t_re - im * t_im, re * t_im + im * t_re
        carry[0, :, cols] = re
        carry[1, :, cols] = im


def angles(delays, first_chan):
    beams = delays.shape[0]
    rows = jnp.transpose(delays.reshape(beams, 8, 2), (2, 1, 0)).reshape(INPUTS, beams)
    factor = 1.0 + first_chan.astype(F32) / CHANNELS
    phase = 2.0 * math.pi * (rows * factor)
    base = jnp.stack([jnp.cos(phase), -jnp.sin(phase)])
    step = (2.0 * math.pi / CHANNELS) * rows
    turn = jnp.stack([jnp.cos(step), -jnp.sin(step)])
    return base, turn


def weights(base, turn, chan_here):
    beams = base.shape[2]
    groups = chan_here // 8
    whole = pl.BlockSpec((2, INPUTS, beams), lambda k: (0, 0, 0))
    return pl.pallas_call(
        weight_kernel,
        grid=(groups // 2,),
        in_specs=[whole, whole],
        out_specs=pl.BlockSpec((2, 256, beams), lambda k: (k, 0, 0)),
        out_shape=jax.ShapeDtypeStruct((groups, 256, beams), BF16),
        scratch_shapes=[pltpu.VMEM((2, INPUTS, beams), F32)],
        compiler_params=pltpu.CompilerParams(vmem_limit_bytes=54 << 20),
        cost_estimate=pl.CostEstimate(flops=20_000_000, bytes_accessed=9_000_000, transcendentals=0),
        name="weights",
    )(base, turn)


def beam_kernel(lag, spec, w_far, out, held, arrived, wide, flat, left, right, l2, l3):
    step = pl.program_id(0)
    slot = lax.rem(step, 2)
    w = held.at[slot]

    def fetch(at, into):
        blocks = w_far.at[pl.ds(at * 4, 4)]
        return pltpu.make_async_copy(blocks, held.at[into], arrived.at[into])

    lane = lax.broadcasted_iota(jnp.int32, (8, LANES), 1) // 32
    chan = lax.broadcasted_iota(jnp.int32, (8, LANES), 0)
    bit0, bit1 = chan % 2 == 1, chan // 2 % 2 == 1
    masks = [jnp.where(chan == lane + 4 * half, 1.0, 0.0).astype(F32) for half in range(2)]

    def spread_out(first_chan, lhs):
        rows = pl.ds(pl.multiple_of(first_chan, 8), 8)
        for four in range(8):
            for v in range(2):
                shifts = []
                for j in range(2):
                    spread = flat[v, j * 8 + four, rows, :]
                    spread = jnp.where(bit0, pltpu.roll(spread, 32, 1), spread)
                    spread = jnp.where(bit1, pltpu.roll(spread, 64, 1), spread)
                    shifts.append(
                        [spread] + [pltpu.roll(spread, 128 - 32 * p, 1) for p in range(1, 4)]
                    )
                for p in range(4):
                    at = (four * 4 + p) * 32 + v * 16
                    for half in range(2):
                        block = jnp.concatenate([shifts[j][p] * masks[half] for j in range(2)], axis=0)
                        lhs[at : at + 16, half * 128 : half * 128 + 128] = block.astype(BF16)

    @pl.when(step == 0)
    def _():
        fetch(0, 0).start()
        wide[0:2048] = spec[...].astype(F32)

        def turn(q, carry):
            j, four = q // 8, q % 8
            straight, crossed = [], []
            for p in range(4):
                row = lax.rem(four * 4 + p + 32 - lag[0], 32) * 8 + j
                got = [wide[pl.ds(row + 2 * r, 8, stride=256), :] for r in range(4)]
                straight += [got[0], got[1], -got[2], -got[3]]
                crossed += [got[2], got[3], got[0], got[1]]
            flat[0, q] = jnp.concatenate(straight, axis=0).T
            flat[1, q] = jnp.concatenate(crossed, axis=0).T
            return carry

        lax.fori_loop(0, 16, turn, 0, unroll=16)

    @pl.when(step + 1 < pl.num_programs(0))
    def _():
        fetch(step + 1, 1 - slot).start()

    fetch(step, slot).wait()

    def form(pair, refs):
        for n in range(4):
            cols = pl.ds(n * 256, 256)
            powers = []
            for group in range(2):
                amp = dot(refs[group][...], w[pair * 2 + group, :, cols])
                powers.append(jnp.sum((amp * amp).reshape(32, 4, 8, 256), axis=1))
            both = jnp.concatenate(powers, axis=1) * (1.0 / INPUTS)
            out[:, 0, pair * 16 : pair * 16 + 16, cols] = both.astype(BF16)

    spread_out(step * 32, left)
    spread_out(step * 32 + 8, right)
    form(0, (left, right))
    spread_out(step * 32 + 16, l2)
    spread_out(step * 32 + 24, l3)
    form(1, (l2, l3))


def beams_of(lag, spec, w, chan_here):
    count = w.shape[2]
    return pl.pallas_call(
        beam_kernel,
        grid=(chan_here // 32,),
        in_specs=[
            pl.BlockSpec(memory_space=pltpu.SMEM),
            pl.BlockSpec(memory_space=pltpu.VMEM),
            pl.BlockSpec(memory_space=pltpu.HBM),
        ],
        out_specs=pl.BlockSpec((32, 1, 32, count), lambda k: (0, 0, k, 0)),
        out_shape=jax.ShapeDtypeStruct((32, 1, chan_here, count), BF16),
        scratch_shapes=[
            pltpu.VMEM((2, 4, 256, count), BF16),
            pltpu.SemaphoreType.DMA((2,)),
            pltpu.VMEM((2304, LANES), F32),
            pltpu.VMEM((2, 16, LANES, LANES), F32),
            pltpu.VMEM((1024, 256), BF16),
            pltpu.VMEM((1024, 256), BF16),
            pltpu.VMEM((1024, 256), BF16),
            pltpu.VMEM((1024, 256), BF16),
        ],
        compiler_params=pltpu.CompilerParams(vmem_limit_bytes=40 << 20),
        cost_estimate=pl.CostEstimate(flops=9_000_000_000, bytes_accessed=17_000_000, transcendentals=0),
        name="beams",
    )(lag, spec, w)


def per_device(voltages, eq_gain, delays):
    frames = voltages.reshape(2, 16, INNER, LANES)
    count = lax.axis_size("shard")
    shard = lax.axis_index("shard")
    place = shard % 2
    halves = frames.reshape(2, 2, 8, INNER, LANES)
    outer = lax.dynamic_slice_in_dim(voltages, place * (8 * LENGTH), 8 * LENGTH, 1)
    outer = outer.reshape(2, 8, INNER, LANES)
    inner = lax.dynamic_index_in_dim(halves, 1 - place, 1, keepdims=False)
    swaps = [(at, (at - 1) % count) for at in range(0, count, 2)]
    far_side = lax.ppermute(outer, "shard", swaps + [(at, at + 1) for at in range(1, count - 1, 2)])
    near_side = lax.ppermute(inner, "shard", [(at, at ^ 1) for at in range(count)])
    keep = jnp.where(shard == count - 1, 0.0, 1.0).astype(F32).reshape(1)
    chan_here = CHANNELS // count
    own = own_part(keep, frames)
    base, turn, gain = lax.optimization_barrier(
        (*angles(delays, shard * chan_here), eq_gain.reshape(2, 32, LANES))
    )
    place = place.astype(jnp.int32).reshape(1)
    messages = front(place, far_side, near_side, own, gain)
    got = lax.all_to_all(
        messages.reshape(256, 8, LANES), ("grp", "shard"), split_axis=0, concat_axis=0, tiled=True
    )
    w = pltpu.with_memory_space_constraint(weights(base, turn, chan_here), pltpu.HBM)
    lag = jnp.where(lax.axis_index("grp") < 4, 1, 0).astype(jnp.int32).reshape(1)
    return beams_of(lag, got.reshape(2048, LANES), w, chan_here)


def solution(mesh):
    placed = (P("grp", "shard"), P("grp", None), P())
    return jax.shard_map(
        per_device,
        mesh=mesh,
        in_specs=placed,
        out_specs=P(None, "grp", "shard", None),
        check_vma=False,
    )
```

```python
import math

import jax
import jax.numpy as jnp
import numpy as np
from jax import lax
from jax.experimental import pallas as pl
from jax.experimental.pallas import tpu as pltpu
from jax.sharding import PartitionSpec as P

CHANNELS = 4096
TAPS = 16
INPUTS = 16
LENGTH = 2 * CHANNELS
INNER = 64
LANES = 128
F32 = jnp.float32
BF16 = jnp.bfloat16


def split(values):
    high = values.astype(np.float32).astype(BF16)
    low = (values - high.astype(np.float64)).astype(np.float32).astype(BF16)
    return high, low


def window_table():
    total = TAPS * LENGTH
    places = np.arange(total, dtype=np.float64)
    centred = (places - (total - 1) / 2.0) / LENGTH
    taper = 0.5 - 0.5 * np.cos(2.0 * math.pi / total * (places + 0.5))
    shaped = np.sinc(centred) * taper
    shaped = shaped / np.sqrt(np.sum(shaped * shaped))
    return shaped.reshape(TAPS, INNER, LANES).astype(np.float32)


def first_table():
    idx = np.arange(INNER)
    phase = 2.0 * math.pi / INNER * (np.outer(idx, idx) % INNER)
    high, low = split(np.concatenate([np.cos(phase), -np.sin(phase)], axis=0))
    return np.concatenate([high, high, low], axis=1)


def twist_table():
    phase = 2.0 * math.pi / LENGTH * np.outer(np.arange(INNER), np.arange(LANES))
    return np.stack([np.cos(phase), -np.sin(phase)]).astype(np.float32)


def second_table():
    k1 = 2 * np.arange(32)[None, :] + np.arange(2)[:, None]
    phase = 2.0 * math.pi / LANES * (np.arange(LANES)[:, None, None] * k1[None] % LANES)
    cos, sin = np.cos(phase), np.sin(phase)
    from_real = np.stack([cos, -sin], axis=2).reshape(LANES, LANES)
    from_imag = np.stack([sin, cos], axis=2).reshape(LANES, LANES)
    return split(np.concatenate([from_real, from_imag], axis=0))[0]


def dot(left, right):
    return jnp.dot(left, right, preferred_element_type=F32)


def parts_of(value):
    high = value.astype(BF16)
    return high, (value - high.astype(F32)).astype(BF16)


def summed(terms):
    lanes = [terms[0], terms[1]] if len(terms) > 1 else [terms[0]]
    for at, term in enumerate(terms[2:]):
        lanes[at % 2] = lanes[at % 2] + term
    return lanes[0] + lanes[1] if len(lanes) > 1 else lanes[0]


def own_kernel(
    keep, own, win_far, first_far, twist_far, second_far,
    partial, win, first, twist, second, wide, arrived,
):
    tables = ((win_far, win), (first_far, first), (twist_far, twist), (second_far, second))
    copies = [
        pltpu.make_async_copy(far, near, arrived.at[at]) for at, (far, near) in enumerate(tables)
    ]
    for copy in copies:
        copy.start()
    for i in range(2):
        wide[i] = own[i].astype(F32)
    for copy in copies:
        copy.wait()
    keep_old = keep[0]

    def filter_step(step, carry):
        i = step // 8
        rows = pl.ds(pl.multiple_of((step % 8) * 8, 8), 8)
        taps = [win[p, rows, :] for p in range(TAPS)]
        xs = [wide[i, t, rows, :] for t in range(16)]
        for t in range(16):
            total = summed([taps[p] * xs[t + p - 7] for p in range(TAPS) if 7 <= t + p < 23])
            partial[i, t, rows, :] = total * keep_old if t >= 8 else total
        return carry

    lax.fori_loop(0, 16, filter_step, 0)


def far(table):
    return pltpu.with_memory_space_constraint(jnp.asarray(table), pltpu.HBM)


def own_part(keep, own):
    args = (
        keep,
        own,
        far(window_table()),
        far(first_table()),
        far(twist_table()),
        far(second_table()),
    )
    return pl.pallas_call(
        own_kernel,
        in_specs=[
            pl.BlockSpec(memory_space=pltpu.SMEM),
            pl.BlockSpec(memory_space=pltpu.VMEM),
        ]
        + [pl.BlockSpec(memory_space=pltpu.HBM)] * 4,
        out_shape=(
            jax.ShapeDtypeStruct((2, 16, INNER, LANES), F32),
            jax.ShapeDtypeStruct((TAPS, INNER, LANES), F32),
            jax.ShapeDtypeStruct((128, 192), BF16),
            jax.ShapeDtypeStruct((2, INNER, LANES), F32),
            jax.ShapeDtypeStruct((256, LANES), BF16),
        ),
        scratch_shapes=[
            pltpu.VMEM((2, 16, INNER, LANES), F32),
            pltpu.SemaphoreType.DMA((4,)),
        ],
        compiler_params=pltpu.CompilerParams(vmem_limit_bytes=24 << 20),
        cost_estimate=pl.CostEstimate(flops=8_000_000, bytes_accessed=3_000_000, transcendentals=0),
        name="own_part",
    )(*args)


def front_kernel(
    place, far_side, near_side, partial, win, first, twist, second, gain, out,
    wide, flt, inter, ready, left,
):
    sends = [
        pltpu.make_async_copy(ready.at[g], out.at[(g + 4) % 8], left.at[g]) for g in range(8)
    ]

    @pl.when(place[0] == 0)
    def _():
        for i in range(2):
            wide[i, 0:7] = far_side[i, 1:8].astype(F32)
            wide[i, 7:15] = near_side[i].astype(F32)

    @pl.when(place[0] != 0)
    def _():
        for i in range(2):
            wide[i, 0:7] = near_side[i, 1:8].astype(F32)
            wide[i, 7:15] = far_side[i].astype(F32)

    def filter_step(step, carry):
        i = step // 8
        rows = pl.ds(pl.multiple_of((step % 8) * 8, 8), 8)
        taps = [win[p, rows, :] for p in range(TAPS)]
        xs = [wide[i, t, rows, :] for t in range(15)]
        for t in range(16):
            total = partial[i, t, rows, :]
            terms = [taps[p] * xs[t + p] for p in range(TAPS) if t + p < 7]
            terms += [taps[p] * xs[t + p - 16] for p in range(TAPS) if t + p >= 23]
            flt[i, t, rows, :] = total + summed(terms) if terms else total
        return carry

    lax.fori_loop(0, 16, filter_step, 0)

    low_lanes = lax.broadcasted_iota(jnp.int32, (64, LANES), 1) < 64

    def group_step(g, carry):
        columns = []
        for i in range(2):
            for j in range(2):
                high, low = parts_of(flt[i, 2 * g + j])
                columns.append(jnp.concatenate([high, low, high], axis=0))
        stage = dot(first[...], jnp.concatenate(columns, axis=1))
        t_re, t_im = twist[0], twist[1]
        turned = []
        for row in range(4):
            re = stage[:64, row * 128 : row * 128 + 128]
            im = stage[64:, row * 128 : row * 128 + 128]
            turned.append(
                jnp.concatenate([re * t_re - im * t_im, re * t_im + im * t_re], axis=1)
            )
        spec = dot(jnp.concatenate(turned, axis=0).astype(BF16), second[...])
        for i in range(2):
            flipped = spec[i * 128 : i * 128 + 128].T
            even, odd = flipped[:64], flipped[64:]
            rows = (
                jnp.where(low_lanes, even, pltpu.roll(odd, 64, 1)),
                jnp.where(low_lanes, pltpu.roll(even, 64, 1), odd),
            )
            for j in range(2):
                for part in range(2):
                    place = part * 4 + i * 2 + j
                    inter[g, pl.ds(place, 32, stride=8), :] = (
                        rows[j][part * 32 : part * 32 + 32] * gain[i]
                    )
        ready[g] = inter[g, 0:256].astype(BF16)
        sends[g].start()
        return carry

    for g in range(8):
        group_step(g, 0)
    for send in sends:
        send.wait()


def front(place, far_side, near_side, own, gain):
    args = (place, far_side, near_side, *own, gain)
    return pl.pallas_call(
        front_kernel,
        in_specs=[pl.BlockSpec(memory_space=pltpu.SMEM)]
        + [pl.BlockSpec(memory_space=pltpu.VMEM)] * 8,
        out_specs=pl.BlockSpec(memory_space=pltpu.HBM),
        out_shape=jax.ShapeDtypeStruct((8, 256, LANES), BF16),
        scratch_shapes=[
            pltpu.VMEM((2, 15, INNER, LANES), F32),
            pltpu.VMEM((2, 16, INNER, LANES), F32),
            pltpu.VMEM((8, 264, LANES), F32),
            pltpu.VMEM((8, 256, LANES), BF16),
            pltpu.SemaphoreType.DMA((8,)),
        ],
        compiler_params=pltpu.CompilerParams(vmem_limit_bytes=24 << 20),
        cost_estimate=pl.CostEstimate(flops=400_000_000, bytes_accessed=3_000_000, transcendentals=0),
        name="front",
    )(*args)


def weight_kernel(base, turn, out, carry):
    @pl.when(pl.program_id(0) == 0)
    def _():
        carry[...] = base[...]

    for block in range(4):
        cols = pl.ds(block * 256, 256)
        re, im = carry[0, :, cols], carry[1, :, cols]
        t_re, t_im = turn[0, :, cols], turn[1, :, cols]
        for c in range(16):
            half, at = c // 8, c % 8 * 32
            out[half, at : at + 16, cols] = re.astype(BF16)
            out[half, at + 16 : at + 32, cols] = im.astype(BF16)
            re, im = re * t_re - im * t_im, re * t_im + im * t_re
        carry[0, :, cols] = re
        carry[1, :, cols] = im


def angles(delays, first_chan):
    beams = delays.shape[0]
    rows = jnp.transpose(delays.reshape(beams, 8, 2), (2, 1, 0)).reshape(INPUTS, beams)
    factor = 1.0 + first_chan.astype(F32) / CHANNELS
    phase = 2.0 * math.pi * (rows * factor)
    base = jnp.stack([jnp.cos(phase), -jnp.sin(phase)])
    step = (2.0 * math.pi / CHANNELS) * rows
    turn = jnp.stack([jnp.cos(step), -jnp.sin(step)])
    return base, turn


def weights(base, turn, chan_here):
    beams = base.shape[2]
    groups = chan_here // 8
    whole = pl.BlockSpec((2, INPUTS, beams), lambda k: (0, 0, 0))
    return pl.pallas_call(
        weight_kernel,
        grid=(groups // 2,),
        in_specs=[whole, whole],
        out_specs=pl.BlockSpec((2, 256, beams), lambda k: (k, 0, 0)),
        out_shape=jax.ShapeDtypeStruct((groups, 256, beams), BF16),
        scratch_shapes=[pltpu.VMEM((2, INPUTS, beams), F32)],
        compiler_params=pltpu.CompilerParams(vmem_limit_bytes=54 << 20),
        cost_estimate=pl.CostEstimate(flops=20_000_000, bytes_accessed=9_000_000, transcendentals=0),
        name="weights",
    )(base, turn)


def beam_kernel(lag, spec, w_far, out, held, arrived, wide, flat, *sides):
    step = pl.program_id(0)
    slot = lax.rem(step, 2)
    w = held.at[slot]

    def fetch(at, into):
        blocks = w_far.at[pl.ds(at * 8, 8)]
        return pltpu.make_async_copy(blocks, held.at[into], arrived.at[into])

    lane = lax.broadcasted_iota(jnp.int32, (8, LANES), 1) // 32
    chan = lax.broadcasted_iota(jnp.int32, (8, LANES), 0)
    bit0, bit1 = chan % 2 == 1, chan // 2 % 2 == 1
    masks = [jnp.where(chan == lane + 4 * half, 1.0, 0.0).astype(F32) for half in range(2)]

    def spread_out(first_chan, lhs):
        rows = pl.ds(pl.multiple_of(first_chan, 8), 8)
        for four in range(8):
            for v in range(2):
                shifts = []
                for j in range(2):
                    spread = flat[v, j * 8 + four, rows, :]
                    spread = jnp.where(bit0, pltpu.roll(spread, 32, 1), spread)
                    spread = jnp.where(bit1, pltpu.roll(spread, 64, 1), spread)
                    shifts.append(
                        [spread] + [pltpu.roll(spread, 128 - 32 * p, 1) for p in range(1, 4)]
                    )
                for p in range(4):
                    at = (four * 4 + p) * 32 + v * 16
                    for half in range(2):
                        block = jnp.concatenate([shifts[j][p] * masks[half] for j in range(2)], axis=0)
                        lhs[at : at + 16, half * 128 : half * 128 + 128] = block.astype(BF16)

    @pl.when(step == 0)
    def _():
        fetch(0, 0).start()
        wide[0:2048] = spec[...].astype(F32)

        def turn(q, carry):
            j, four = q // 8, q % 8
            straight, crossed = [], []
            for p in range(4):
                row = lax.rem(four * 4 + p + 32 - lag[0], 32) * 8 + j
                got = [wide[pl.ds(row + 2 * r, 8, stride=256), :] for r in range(4)]
                straight += [got[0], got[1], -got[2], -got[3]]
                crossed += [got[2], got[3], got[0], got[1]]
            flat[0, q] = jnp.concatenate(straight, axis=0).T
            flat[1, q] = jnp.concatenate(crossed, axis=0).T
            return carry

        lax.fori_loop(0, 16, turn, 0, unroll=16)

    @pl.when(step + 1 < pl.num_programs(0))
    def _():
        fetch(step + 1, 1 - slot).start()

    fetch(step, slot).wait()

    def form(pair, refs):
        for n in range(4):
            cols = pl.ds(n * 256, 256)
            powers = []
            for group in range(2):
                amp = dot(refs[group][...], w[pair * 2 + group, :, cols])
                powers.append(jnp.sum((amp * amp).reshape(32, 4, 8, 256), axis=1))
            both = jnp.concatenate(powers, axis=1) * (1.0 / INPUTS)
            out[:, 0, pair * 16 : pair * 16 + 16, cols] = both.astype(BF16)

    for pair in range(4):
        refs = sides[2 * pair : 2 * pair + 2]
        for group in range(2):
            spread_out(step * 64 + pair * 16 + group * 8, refs[group])
        form(pair, refs)


def beams_of(lag, spec, w, chan_here):
    count = w.shape[2]
    return pl.pallas_call(
        beam_kernel,
        grid=(chan_here // 64,),
        in_specs=[
            pl.BlockSpec(memory_space=pltpu.SMEM),
            pl.BlockSpec(memory_space=pltpu.VMEM),
            pl.BlockSpec(memory_space=pltpu.HBM),
        ],
        out_specs=pl.BlockSpec((32, 1, 64, count), lambda k: (0, 0, k, 0)),
        out_shape=jax.ShapeDtypeStruct((32, 1, chan_here, count), BF16),
        scratch_shapes=[
            pltpu.VMEM((2, 8, 256, count), BF16),
            pltpu.SemaphoreType.DMA((2,)),
            pltpu.VMEM((2304, LANES), F32),
            pltpu.VMEM((2, 16, LANES, LANES), F32),
        ]
        + [pltpu.VMEM((1024, 256), BF16)] * 8,
        compiler_params=pltpu.CompilerParams(vmem_limit_bytes=40 << 20),
        cost_estimate=pl.CostEstimate(flops=9_000_000_000, bytes_accessed=17_000_000, transcendentals=0),
        name="beams",
    )(lag, spec, w)


def per_device(voltages, eq_gain, delays):
    frames = voltages.reshape(2, 16, INNER, LANES)
    count = lax.axis_size("shard")
    shard = lax.axis_index("shard")
    place = shard % 2
    halves = frames.reshape(2, 2, 8, INNER, LANES)
    outer = lax.dynamic_slice_in_dim(voltages, place * (8 * LENGTH), 8 * LENGTH, 1)
    outer = outer.reshape(2, 8, INNER, LANES)
    inner = lax.dynamic_index_in_dim(halves, 1 - place, 1, keepdims=False)
    swaps = [(at, (at - 1) % count) for at in range(0, count, 2)]
    far_side = lax.ppermute(outer, "shard", swaps + [(at, at + 1) for at in range(1, count - 1, 2)])
    near_side = lax.ppermute(inner, "shard", [(at, at ^ 1) for at in range(count)])
    keep = jnp.where(shard == count - 1, 0.0, 1.0).astype(F32).reshape(1)
    chan_here = CHANNELS // count
    own = own_part(keep, frames)
    base, turn, gain = lax.optimization_barrier(
        (*angles(delays, shard * chan_here), eq_gain.reshape(2, 32, LANES))
    )
    place = place.astype(jnp.int32).reshape(1)
    messages = front(place, far_side, near_side, own, gain)
    got = lax.all_to_all(
        messages.reshape(256, 8, LANES), ("grp", "shard"), split_axis=0, concat_axis=0, tiled=True
    )
    w = pltpu.with_memory_space_constraint(weights(base, turn, chan_here), pltpu.HBM)
    lag = jnp.where(lax.axis_index("grp") < 4, 1, 0).astype(jnp.int32).reshape(1)
    return beams_of(lag, got.reshape(2048, LANES), w, chan_here)


def solution(mesh):
    placed = (P("grp", "shard"), P("grp", None), P())
    return jax.shard_map(
        per_device,
        mesh=mesh,
        in_specs=placed,
        out_specs=P(None, "grp", "shard", None),
        check_vma=False,
    )
```

```python
import math

import jax
import jax.numpy as jnp
import numpy as np
from jax import lax
from jax.experimental import pallas as pl
from jax.experimental.pallas import tpu as pltpu
from jax.sharding import PartitionSpec as P

CHANNELS = 4096
TAPS = 16
INPUTS = 16
LENGTH = 2 * CHANNELS
INNER = 64
LANES = 128
F32 = jnp.float32
BF16 = jnp.bfloat16


def split(values):
    high = values.astype(np.float32).astype(BF16)
    low = (values - high.astype(np.float64)).astype(np.float32).astype(BF16)
    return high, low


def window_table():
    total = TAPS * LENGTH
    places = np.arange(total, dtype=np.float64)
    centred = (places - (total - 1) / 2.0) / LENGTH
    taper = 0.5 - 0.5 * np.cos(2.0 * math.pi / total * (places + 0.5))
    shaped = np.sinc(centred) * taper
    shaped = shaped / np.sqrt(np.sum(shaped * shaped))
    return shaped.reshape(TAPS, INNER, LANES).astype(np.float32)


def first_table():
    idx = np.arange(INNER)
    phase = 2.0 * math.pi / INNER * (np.outer(idx, idx) % INNER)
    high, low = split(np.concatenate([np.cos(phase), -np.sin(phase)], axis=0))
    return np.concatenate([high, high, low], axis=1)


def twist_table():
    phase = 2.0 * math.pi / LENGTH * np.outer(np.arange(INNER), np.arange(LANES))
    return np.stack([np.cos(phase), -np.sin(phase)]).astype(np.float32)


def second_table():
    k1 = 2 * np.arange(32)[None, :] + np.arange(2)[:, None]
    phase = 2.0 * math.pi / LANES * (np.arange(LANES)[:, None, None] * k1[None] % LANES)
    cos, sin = np.cos(phase), np.sin(phase)
    from_real = np.stack([cos, -sin], axis=2).reshape(LANES, LANES)
    from_imag = np.stack([sin, cos], axis=2).reshape(LANES, LANES)
    return split(np.concatenate([from_real, from_imag], axis=0))[0]


def dot(left, right):
    return jnp.dot(left, right, preferred_element_type=F32)


def parts_of(value):
    high = value.astype(BF16)
    return high, (value - high.astype(F32)).astype(BF16)


def summed(terms):
    lanes = [terms[0], terms[1]] if len(terms) > 1 else [terms[0]]
    for at, term in enumerate(terms[2:]):
        lanes[at % 2] = lanes[at % 2] + term
    return lanes[0] + lanes[1] if len(lanes) > 1 else lanes[0]


def own_kernel(
    keep, own, win_far, first_far, twist_far, second_far,
    partial, win, first, twist, second, wide, arrived,
):
    tables = ((win_far, win), (first_far, first), (twist_far, twist), (second_far, second))
    copies = [
        pltpu.make_async_copy(far, near, arrived.at[at]) for at, (far, near) in enumerate(tables)
    ]
    for copy in copies:
        copy.start()
    for i in range(2):
        wide[i] = own[i].astype(F32)
    for copy in copies:
        copy.wait()
    keep_old = keep[0]

    def filter_step(step, carry):
        i = step // 8
        rows = pl.ds(pl.multiple_of((step % 8) * 8, 8), 8)
        taps = [win[p, rows, :] for p in range(TAPS)]
        xs = [wide[i, t, rows, :] for t in range(16)]
        for t in range(16):
            total = summed([taps[p] * xs[t + p - 7] for p in range(TAPS) if 7 <= t + p < 23])
            partial[i, t, rows, :] = total * keep_old if t >= 8 else total
        return carry

    lax.fori_loop(0, 16, filter_step, 0)


def far(table):
    return pltpu.with_memory_space_constraint(jnp.asarray(table), pltpu.HBM)


def own_part(keep, own):
    args = (
        keep,
        own,
        far(window_table()),
        far(first_table()),
        far(twist_table()),
        far(second_table()),
    )
    return pl.pallas_call(
        own_kernel,
        in_specs=[
            pl.BlockSpec(memory_space=pltpu.SMEM),
            pl.BlockSpec(memory_space=pltpu.VMEM),
        ]
        + [pl.BlockSpec(memory_space=pltpu.HBM)] * 4,
        out_shape=(
            jax.ShapeDtypeStruct((2, 16, INNER, LANES), F32),
            jax.ShapeDtypeStruct((TAPS, INNER, LANES), F32),
            jax.ShapeDtypeStruct((128, 192), BF16),
            jax.ShapeDtypeStruct((2, INNER, LANES), F32),
            jax.ShapeDtypeStruct((256, LANES), BF16),
        ),
        scratch_shapes=[
            pltpu.VMEM((2, 16, INNER, LANES), F32),
            pltpu.SemaphoreType.DMA((4,)),
        ],
        compiler_params=pltpu.CompilerParams(vmem_limit_bytes=24 << 20),
        cost_estimate=pl.CostEstimate(flops=8_000_000, bytes_accessed=3_000_000, transcendentals=0),
        name="own_part",
    )(*args)


def front_kernel(
    place, far_side, near_side, partial, win, first, twist, second, gain, out,
    wide, flt, inter, ready, left,
):
    sends = [
        pltpu.make_async_copy(ready.at[g], out.at[(g + 4) % 8], left.at[g]) for g in range(8)
    ]

    @pl.when(place[0] == 0)
    def _():
        for i in range(2):
            wide[i, 0:7] = far_side[i, 1:8].astype(F32)
            wide[i, 7:15] = near_side[i].astype(F32)

    @pl.when(place[0] != 0)
    def _():
        for i in range(2):
            wide[i, 0:7] = near_side[i, 1:8].astype(F32)
            wide[i, 7:15] = far_side[i].astype(F32)

    def filter_step(step, carry):
        i = step // 8
        rows = pl.ds(pl.multiple_of((step % 8) * 8, 8), 8)
        taps = [win[p, rows, :] for p in range(TAPS)]
        xs = [wide[i, t, rows, :] for t in range(15)]
        for t in range(16):
            total = partial[i, t, rows, :]
            terms = [taps[p] * xs[t + p] for p in range(TAPS) if t + p < 7]
            terms += [taps[p] * xs[t + p - 16] for p in range(TAPS) if t + p >= 23]
            flt[i, t, rows, :] = total + summed(terms) if terms else total
        return carry

    lax.fori_loop(0, 16, filter_step, 0, unroll=4)

    low_lanes = lax.broadcasted_iota(jnp.int32, (64, LANES), 1) < 64

    def group_step(g, carry):
        columns = []
        for i in range(2):
            for j in range(2):
                high, low = parts_of(flt[i, 2 * g + j])
                columns.append(jnp.concatenate([high, low, high], axis=0))
        stage = dot(first[...], jnp.concatenate(columns, axis=1))
        t_re, t_im = twist[0], twist[1]
        turned = []
        for row in range(4):
            re = stage[:64, row * 128 : row * 128 + 128]
            im = stage[64:, row * 128 : row * 128 + 128]
            turned.append(
                jnp.concatenate([re * t_re - im * t_im, re * t_im + im * t_re], axis=1)
            )
        spec = dot(jnp.concatenate(turned, axis=0).astype(BF16), second[...])
        for i in range(2):
            flipped = spec[i * 128 : i * 128 + 128].T
            even, odd = flipped[:64], flipped[64:]
            rows = (
                jnp.where(low_lanes, even, pltpu.roll(odd, 64, 1)),
                jnp.where(low_lanes, pltpu.roll(even, 64, 1), odd),
            )
            for j in range(2):
                for part in range(2):
                    place = part * 4 + i * 2 + j
                    inter[g, pl.ds(place, 32, stride=8), :] = (
                        rows[j][part * 32 : part * 32 + 32] * gain[i]
                    )
        ready[g] = inter[g, 0:256].astype(BF16)
        sends[g].start()
        return carry

    for g in range(8):
        group_step(g, 0)
    for send in sends:
        send.wait()


def front(place, far_side, near_side, own, gain):
    args = (place, far_side, near_side, *own, gain)
    return pl.pallas_call(
        front_kernel,
        in_specs=[pl.BlockSpec(memory_space=pltpu.SMEM)]
        + [pl.BlockSpec(memory_space=pltpu.VMEM)] * 8,
        out_specs=pl.BlockSpec(memory_space=pltpu.HBM),
        out_shape=jax.ShapeDtypeStruct((8, 256, LANES), BF16),
        scratch_shapes=[
            pltpu.VMEM((2, 15, INNER, LANES), F32),
            pltpu.VMEM((2, 16, INNER, LANES), F32),
            pltpu.VMEM((8, 264, LANES), F32),
            pltpu.VMEM((8, 256, LANES), BF16),
            pltpu.SemaphoreType.DMA((8,)),
        ],
        compiler_params=pltpu.CompilerParams(vmem_limit_bytes=24 << 20),
        cost_estimate=pl.CostEstimate(flops=400_000_000, bytes_accessed=3_000_000, transcendentals=0),
        name="front",
    )(*args)


def weight_kernel(base, turn, out, carry):
    @pl.when(pl.program_id(0) == 0)
    def _():
        carry[...] = base[...]

    for block in range(4):
        cols = pl.ds(block * 256, 256)
        re, im = carry[0, :, cols], carry[1, :, cols]
        t_re, t_im = turn[0, :, cols], turn[1, :, cols]
        for c in range(16):
            half, at = c // 8, c % 8 * 32
            out[half, at : at + 16, cols] = re.astype(BF16)
            out[half, at + 16 : at + 32, cols] = im.astype(BF16)
            re, im = re * t_re - im * t_im, re * t_im + im * t_re
        carry[0, :, cols] = re
        carry[1, :, cols] = im


def angles(delays, first_chan):
    beams = delays.shape[0]
    rows = jnp.transpose(delays.reshape(beams, 8, 2), (2, 1, 0)).reshape(INPUTS, beams)
    factor = 1.0 + first_chan.astype(F32) / CHANNELS
    phase = 2.0 * math.pi * (rows * factor)
    base = jnp.stack([jnp.cos(phase), -jnp.sin(phase)])
    step = (2.0 * math.pi / CHANNELS) * rows
    turn = jnp.stack([jnp.cos(step), -jnp.sin(step)])
    return base, turn


def weights(base, turn, chan_here):
    beams = base.shape[2]
    groups = chan_here // 8
    whole = pl.BlockSpec((2, INPUTS, beams), lambda k: (0, 0, 0))
    return pl.pallas_call(
        weight_kernel,
        grid=(groups // 2,),
        in_specs=[whole, whole],
        out_specs=pl.BlockSpec((2, 256, beams), lambda k: (k, 0, 0)),
        out_shape=jax.ShapeDtypeStruct((groups, 256, beams), BF16),
        scratch_shapes=[pltpu.VMEM((2, INPUTS, beams), F32)],
        compiler_params=pltpu.CompilerParams(vmem_limit_bytes=54 << 20),
        cost_estimate=pl.CostEstimate(flops=20_000_000, bytes_accessed=9_000_000, transcendentals=0),
        name="weights",
    )(base, turn)


def beam_kernel(lag, spec, w_far, out, held, arrived, wide, flat, left, right, l2, l3):
    step = pl.program_id(0)
    slot = lax.rem(step, 2)
    w = held.at[slot]

    def fetch(at, into):
        blocks = w_far.at[pl.ds(at * 4, 4)]
        return pltpu.make_async_copy(blocks, held.at[into], arrived.at[into])

    lane = lax.broadcasted_iota(jnp.int32, (8, LANES), 1) // 32
    chan = lax.broadcasted_iota(jnp.int32, (8, LANES), 0)
    bit0, bit1 = chan % 2 == 1, chan // 2 % 2 == 1
    masks = [jnp.where(chan == lane + 4 * half, 1.0, 0.0).astype(F32) for half in range(2)]

    def spread_out(first_chan, lhs):
        rows = pl.ds(pl.multiple_of(first_chan, 8), 8)
        for four in range(8):
            for v in range(2):
                shifts = []
                for j in range(2):
                    spread = flat[v, j * 8 + four, rows, :]
                    spread = jnp.where(bit0, pltpu.roll(spread, 32, 1), spread)
                    spread = jnp.where(bit1, pltpu.roll(spread, 64, 1), spread)
                    shifts.append(
                        [spread] + [pltpu.roll(spread, 128 - 32 * p, 1) for p in range(1, 4)]
                    )
                for p in range(4):
                    at = (four * 4 + p) * 32 + v * 16
                    for half in range(2):
                        block = jnp.concatenate([shifts[j][p] * masks[half] for j in range(2)], axis=0)
                        lhs[at : at + 16, half * 128 : half * 128 + 128] = block.astype(BF16)

    @pl.when(step == 0)
    def _():
        fetch(0, 0).start()
        wide[0:2048] = spec[...].astype(F32)

        def turn(q, carry):
            j, four = q // 8, q % 8
            straight, crossed = [], []
            for p in range(4):
                row = lax.rem(four * 4 + p + 32 - lag[0], 32) * 8 + j
                got = [wide[pl.ds(row + 2 * r, 8, stride=256), :] for r in range(4)]
                straight += [got[0], got[1], -got[2], -got[3]]
                crossed += [got[2], got[3], got[0], got[1]]
            flat[0, q] = jnp.concatenate(straight, axis=0).T
            flat[1, q] = jnp.concatenate(crossed, axis=0).T
            return carry

        lax.fori_loop(0, 16, turn, 0, unroll=16)

    @pl.when(step + 1 < pl.num_programs(0))
    def _():
        fetch(step + 1, 1 - slot).start()

    fetch(step, slot).wait()

    def form(pair, refs):
        for n in range(4):
            cols = pl.ds(n * 256, 256)
            powers = []
            for group in range(2):
                amp = dot(refs[group][...], w[pair * 2 + group, :, cols])
                powers.append(jnp.sum((amp * amp).reshape(32, 4, 8, 256), axis=1))
            both = jnp.concatenate(powers, axis=1) * (1.0 / INPUTS)
            out[:, 0, pair * 16 : pair * 16 + 16, cols] = both.astype(BF16)

    spread_out(step * 32, left)
    spread_out(step * 32 + 8, right)
    form(0, (left, right))
    spread_out(step * 32 + 16, l2)
    spread_out(step * 32 + 24, l3)
    form(1, (l2, l3))


def beams_of(lag, spec, w, chan_here):
    count = w.shape[2]
    return pl.pallas_call(
        beam_kernel,
        grid=(chan_here // 32,),
        in_specs=[
            pl.BlockSpec(memory_space=pltpu.SMEM),
            pl.BlockSpec(memory_space=pltpu.VMEM),
            pl.BlockSpec(memory_space=pltpu.HBM),
        ],
        out_specs=pl.BlockSpec((32, 1, 32, count), lambda k: (0, 0, k, 0)),
        out_shape=jax.ShapeDtypeStruct((32, 1, chan_here, count), BF16),
        scratch_shapes=[
            pltpu.VMEM((2, 4, 256, count), BF16),
            pltpu.SemaphoreType.DMA((2,)),
            pltpu.VMEM((2304, LANES), F32),
            pltpu.VMEM((2, 16, LANES, LANES), F32),
            pltpu.VMEM((1024, 256), BF16),
            pltpu.VMEM((1024, 256), BF16),
            pltpu.VMEM((1024, 256), BF16),
            pltpu.VMEM((1024, 256), BF16),
        ],
        compiler_params=pltpu.CompilerParams(vmem_limit_bytes=40 << 20),
        cost_estimate=pl.CostEstimate(flops=9_000_000_000, bytes_accessed=17_000_000, transcendentals=0),
        name="beams",
    )(lag, spec, w)


def per_device(voltages, eq_gain, delays):
    frames = voltages.reshape(2, 16, INNER, LANES)
    count = lax.axis_size("shard")
    shard = lax.axis_index("shard")
    place = shard % 2
    halves = frames.reshape(2, 2, 8, INNER, LANES)
    outer = lax.dynamic_slice_in_dim(voltages, place * (8 * LENGTH), 8 * LENGTH, 1)
    outer = outer.reshape(2, 8, INNER, LANES)
    inner = lax.dynamic_index_in_dim(halves, 1 - place, 1, keepdims=False)
    swaps = [(at, (at - 1) % count) for at in range(0, count, 2)]
    far_side = lax.ppermute(outer, "shard", swaps + [(at, at + 1) for at in range(1, count - 1, 2)])
    near_side = lax.ppermute(inner, "shard", [(at, at ^ 1) for at in range(count)])
    keep = jnp.where(shard == count - 1, 0.0, 1.0).astype(F32).reshape(1)
    chan_here = CHANNELS // count
    own = own_part(keep, frames)
    base, turn, gain = lax.optimization_barrier(
        (*angles(delays, shard * chan_here), eq_gain.reshape(2, 32, LANES))
    )
    place = place.astype(jnp.int32).reshape(1)
    messages = front(place, far_side, near_side, own, gain)
    got = lax.all_to_all(
        messages.reshape(256, 8, LANES), ("grp", "shard"), split_axis=0, concat_axis=0, tiled=True
    )
    w = pltpu.with_memory_space_constraint(weights(base, turn, chan_here), pltpu.HBM)
    lag = jnp.where(lax.axis_index("grp") < 4, 1, 0).astype(jnp.int32).reshape(1)
    return beams_of(lag, got.reshape(2048, LANES), w, chan_here)


def solution(mesh):
    placed = (P("grp", "shard"), P("grp", None), P())
    return jax.shard_map(
        per_device,
        mesh=mesh,
        in_specs=placed,
        out_specs=P(None, "grp", "shard", None),
        check_vma=False,
    )
```
